32 devices in a mesh: blk: 16 (over z, y, core), rep: 2 (over x).
Axes of the slice: x: 2, y: 2, z: 4, core: 2. Of those that a mesh axis runs over, the one named last changes fastest.
Arguments:
- samples: bfloat16 [512, 16, 2048], P('blk', 'rep'), may hold values from -60 to 60, as said below
- offsets: int32 [4, 512], P(None, 'blk'), may hold values from 0 to 31
- bad_mask: int32 [512], P('blk'), may hold values 0 or 1
Outputs:
- correlations: float32 [512, 4, 257], P('blk')
- mirrored: float32 [512, 4, 257], P('blk')
The draws below stay inside these ranges and needn't reach their ends.
Inputs may be any that keep to these rules, and one draw needn't show every extreme that they name: `samples`: samples vary in scale between channels and segments; channels near one another share a delayed common source.
All inputs are finite; a program needn't handle non-finite values. No bound on the sum of `bad_mask` on one device may be relied on, other than what follows from the above.
Results may differ from the reference program's by a relative error of at most 0.0017.
Values may be sent and summed in bfloat16 or wider, within the bound.
A program may use at most 64 MiB of HBM per device.

```python
import math
import jax
import jax.numpy as jnp
from jax import lax

CH_DEV = 32
NS = 2048
LAGS = 128
STOPS = 4
NF = 1024
LAGW = 257
CHANNELS = 512
NSEG = 16
N_BLK = 16


def draw_samples(key, part):
    key_scale, key_own, key_common = jax.random.split(key, 3)
    scales = jnp.exp(jax.random.uniform(key_scale, (CHANNELS, NSEG, 1), jnp.float32, math.log(0.1), math.log(10.0)))
    own = jax.random.normal(key_own, (CHANNELS, NSEG, NS), jnp.float32)
    common = jax.random.normal(key_common, (NSEG, NS), jnp.float32)
    delays = jnp.arange(CHANNELS, dtype=jnp.int32) * 37 % 97
    where = (jnp.arange(NS, dtype=jnp.int32)[None, :] - delays[:, None]) % NS
    shared = jnp.transpose(common[:, where], (1, 0, 2))
    values = scales * (own + 0.8 * shared)
    return jnp.clip(values, -60.0, 60.0).astype(jnp.bfloat16)


def place_ends(entries, rng, low, high):
    shape = entries.shape
    place = [jax.random.randint(jax.random.fold_in(rng, axis), (), 0, shape[axis]) for axis in range(len(shape))]
    entries = entries.at[tuple(place)].set(low)
    longest = shape.index(max(shape))
    place[longest] = (place[longest] + 1) % shape[longest]
    return entries.at[tuple(place)].set(high)


def setup_inputs(seed: int = 0) -> dict:
    splits = jax.random.split(jax.random.key(seed), 4)
    return {
        "samples": draw_samples(jax.random.fold_in(splits[3], 71), 0),
        "offsets": place_ends(jax.random.randint(splits[1], (STOPS, CHANNELS), 0, CH_DEV), jax.random.fold_in(splits[1], 1), 0, CH_DEV - 1).astype(jnp.int32),
        "bad_mask": place_ends((jax.random.randint(splits[2], (CHANNELS,), 0, 8) < 1).astype(jnp.int32), jax.random.fold_in(splits[2], 1), 0, 1),
    }


def forward_table(length):
    half_len = length // 2
    sample_idx = lax.iota(jnp.int32, length)
    bin_idx = lax.iota(jnp.int32, half_len)
    phase = sample_idx[:, None] * bin_idx[None, :] % length
    angle = phase.astype(jnp.float32) * (2.0 * math.pi / length)
    return jnp.concatenate([jnp.cos(angle), -jnp.sin(angle)], axis=1).astype(jnp.bfloat16)

def inverse_table(length, lag_half):
    half_len = length // 2
    bin_idx = lax.iota(jnp.int32, half_len)
    lag_idx = lax.iota(jnp.int32, 2 * lag_half + 1) - lag_half
    phase = bin_idx[:, None] * (lag_idx[None, :] % length) % length
    angle = phase.astype(jnp.float32) * (2.0 * math.pi / length)
    return jnp.concatenate([jnp.cos(angle), -jnp.sin(angle)], axis=0)

def whiten(spectrum, keep, half_len):
    power = lax.optimization_barrier(jnp.sum(spectrum * spectrum, axis=-1, keepdims=True)) / half_len
    return (spectrum * lax.rsqrt(power + 1e-06) * keep[:, None, None]).astype(jnp.bfloat16)

def cross_spectrum(local, partner, half_len):
    first = local.astype(jnp.float32)
    second = partner.astype(jnp.float32)
    real_a, imag_a = (first[..., :half_len], first[..., half_len:])
    real_b, imag_b = (second[..., :half_len], second[..., half_len:])
    real_sum = lax.optimization_barrier(jnp.sum(real_a * real_b + imag_a * imag_b, axis=1))
    imag_sum = lax.optimization_barrier(jnp.sum(imag_a * real_b - real_a * imag_b, axis=1))
    return jnp.concatenate([real_sum, imag_sum], axis=-1)

def reference(samples, offsets, bad_mask):
    table = forward_table(NS).astype(jnp.float32)
    back_table = inverse_table(NS, LAGS)
    keep = (1 - bad_mask).astype(jnp.float32)
    scale = 1.0 / math.sqrt(NSEG * NF)

    def one_block(block):
        start = (block * CH_DEV).astype(jnp.int32)
        rows = lax.dynamic_slice_in_dim(samples, start, CH_DEV, 0).astype(jnp.float32)
        spectrum = jnp.dot(rows.reshape(CH_DEV * NSEG, NS), table, precision=lax.Precision.HIGHEST, preferred_element_type=jnp.float32).reshape(CH_DEV, NSEG, NS)
        return whiten(spectrum, lax.dynamic_slice_in_dim(keep, start, CH_DEV, 0), NF)
    blocks = jnp.arange(N_BLK, dtype=jnp.int32)
    white = lax.map(one_block, blocks).reshape(CHANNELS, NSEG, NS)

    def block_corr(block):
        start = (block * CH_DEV).astype(jnp.int32)
        local = lax.dynamic_slice_in_dim(white, start, CH_DEV, 0)
        pieces = []
        for stop in range(1, STOPS + 1):
            source = ((block - stop) % N_BLK * CH_DEV).astype(jnp.int32)
            remote = lax.dynamic_slice_in_dim(white, source, CH_DEV, 0)
            picks = lax.dynamic_slice_in_dim(offsets[stop - 1], start, CH_DEV, 0)
            partner = jnp.take(remote, picks, axis=0)
            pieces.append(cross_spectrum(local, partner, NF))
        cross = jnp.stack(pieces, axis=1)
        corr = jnp.dot(cross.reshape(CH_DEV * STOPS, NS), back_table, precision=lax.Precision.HIGHEST, preferred_element_type=jnp.float32)
        return corr.reshape(CH_DEV, STOPS, LAGW) * scale
    correlations = lax.map(block_corr, blocks).reshape(CHANNELS, STOPS, LAGW)
    stop_idx = jnp.arange(STOPS, dtype=jnp.int32)
    owner = (jnp.arange(CHANNELS, dtype=jnp.int32)[:, None] + (stop_idx[None, :] + 1) * CH_DEV) % CHANNELS
    mirrored = correlations[owner, stop_idx[None, :], :][:, :, ::-1]
    return (correlations, mirrored)
```

```python
import math

import jax
import jax.numpy as jnp
import ml_dtypes
import numpy as np
from jax import lax
from jax.sharding import PartitionSpec as P

LAGS = 128


def shifted(x, axis, by):
    length = lax.axis_size(axis)
    return lax.ppermute(x, axis, [(i, (i + by) % length) for i in range(length)])


def forward_table(length):
    phase = np.arange(length)[:, None] * np.arange(length // 2)[None, :] % length
    angle = phase * (2.0 * math.pi / length)
    return np.concatenate([np.cos(angle), -np.sin(angle)], axis=1).astype(ml_dtypes.bfloat16)


def inverse_table(length, lag_half):
    lag_idx = np.arange(2 * lag_half + 1) - lag_half
    phase = np.arange(length // 2)[:, None] * (lag_idx[None, :] % length) % length
    angle = phase * (2.0 * math.pi / length)
    return np.concatenate([np.cos(angle), -np.sin(angle)], axis=0).astype(np.float32)


def whiten(spectrum, keep, half_len):
    power = jnp.sum(spectrum * spectrum, axis=-1, keepdims=True) / half_len
    return (spectrum * lax.rsqrt(power + 1e-06) * keep[:, None, None]).astype(jnp.bfloat16)


def cross_spectrum(local, partner, half_len):
    first = local.astype(jnp.float32)
    second = partner.astype(jnp.float32)
    real_a, imag_a = (first[..., :half_len], first[..., half_len:])
    real_b, imag_b = (second[..., :half_len], second[..., half_len:])
    real_sum = jnp.sum(real_a * real_b + imag_a * imag_b, axis=1)
    imag_sum = jnp.sum(imag_a * real_b - real_a * imag_b, axis=1)
    return jnp.concatenate([real_sum, imag_sum], axis=-1)


def on_device(samples, offsets, bad_mask):
    channels, segments, length = samples.shape
    half_len = length // 2
    stops = offsets.shape[0]
    spectrum = jnp.dot(
        samples.reshape(channels * segments, length),
        jnp.asarray(forward_table(length)),
        preferred_element_type=jnp.float32,
    ).reshape(channels, segments, length)
    keep = (1 - bad_mask).astype(jnp.float32)
    white = whiten(spectrum, keep, half_len)
    pieces = []
    moving = white
    for stop in range(1, stops + 1):
        moving = shifted(moving, "blk", 1)
        partner = jnp.take(moving, offsets[stop - 1], axis=0)
        pieces.append(cross_spectrum(white, partner, half_len))
    cross = jnp.stack(pieces, axis=1)
    scale = 1.0 / math.sqrt(segments * lax.axis_size("rep") * half_len)
    partial = jnp.dot(
        cross.reshape(channels * stops, length),
        jnp.asarray(inverse_table(length, LAGS)),
        precision=lax.Precision.HIGHEST,
        preferred_element_type=jnp.float32,
    ).reshape(channels, stops, -1)
    correlations = lax.psum(partial, "rep") * scale
    mirrored = []
    for stop in range(1, stops + 1):
        flipped = correlations[:, stop - 1, ::-1]
        mirrored.append(shifted(flipped, "blk", -stop))
    return (correlations, jnp.stack(mirrored, axis=1))


def solution(mesh):
    return jax.shard_map(
        on_device,
        mesh=mesh,
        in_specs=(P("blk", "rep", None), P(None, "blk"), P("blk")),
        out_specs=(P("blk", None, None), P("blk", None, None)),
        check_vma=False,
    )
```

```python
import functools
import math

import jax
import jax.numpy as jnp
import ml_dtypes
import numpy as np
from jax import lax
from jax.experimental import pallas as pl
from jax.experimental.pallas import tpu as pltpu
from jax.sharding import PartitionSpec as P

LAGS = 128
LANES = 128
MESH = pl.DeviceIdType.MESH
F32 = jnp.float32
BF16 = jnp.bfloat16


def forward_table(length, bins):
    phase = np.arange(length)[:, None] * np.arange(length // 2)[None, :] % length
    angle = phase * (2.0 * math.pi / length)
    real = np.cos(angle).reshape(length, -1, bins)
    imag = -np.sin(angle).reshape(length, -1, bins)
    both = np.concatenate([real, imag], axis=2).transpose(1, 0, 2)
    return np.ascontiguousarray(both).astype(ml_dtypes.bfloat16)


def inverse_table(length, lag_half, bins, padded):
    width = 2 * lag_half + 1
    lag_idx = np.arange(width) - lag_half
    phase = np.arange(length // 2)[:, None] * (lag_idx[None, :] % length) % length
    angle = phase * (2.0 * math.pi / length)
    whole = np.zeros((2, length // 2, padded), np.float32)
    whole[0, :, :width] = np.cos(angle)
    whole[1, :, :width] = np.sin(angle)
    high = whole.astype(ml_dtypes.bfloat16)
    low = (whole - high.astype(np.float32)).astype(ml_dtypes.bfloat16)
    both = np.stack([high, low], axis=1).reshape(2, 2, -1, bins, padded)
    return np.ascontiguousarray(both.transpose(2, 0, 1, 3, 4))


def kernel(
    scale,
    groups,
    samples, table, back, offsets, bad,
    corr, mirr,
    table_v, back_v, spec, norm, own, part, peer, even, odd_, flip,
    table_sem, back_sem, send_sem, recv_sem, rep_send, rep_recv, mir_send, mir_recv,
    *far_flat,
):
    stops, channels, padded = corr.shape
    rows = samples.shape[0]
    segs = rows // channels
    bins = own.shape[-1]
    far = [far_flat[d * groups:(d + 1) * groups] for d in range(stops)]
    blk, rep = lax.axis_index("blk"), lax.axis_index("rep")
    n = lax.axis_size("blk")
    core = lax.rem(blk, 2)
    odd = lax.rem(blk // 2, 2)
    up = lax.rem(blk + 4, n)
    beside = blk + 2 - 4 * odd
    sibling = blk + 1 - 2 * core
    other = 1 - rep

    def load(j):
        return pltpu.make_async_copy(table.at[j], table_v.at[j], table_sem.at[j])

    for j in range(groups):
        load(j).start()
    back_load = pltpu.make_async_copy(back, back_v, back_sem)
    back_load.start()

    barrier = pltpu.get_barrier_semaphore()
    for by in range(1, stops + 1):
        for who in (lax.rem(blk + by, n), lax.rem(blk + n - by, n)):
            pl.semaphore_signal(barrier, inc=1, device_id=(who, rep), device_id_type=MESH)
    pl.semaphore_signal(barrier, inc=1, device_id=(blk, other), device_id_type=MESH)
    pl.semaphore_wait(barrier, 2 * stops + 1)

    def send(src, stop, k, lane, who):
        return pltpu.make_async_remote_copy(
            src_ref=src,
            dst_ref=far[stop - 1][k],
            send_sem=send_sem.at[lane, k],
            recv_sem=recv_sem.at[stop - 1, k],
            device_id=(who, rep),
            device_id_type=MESH,
        )

    def arrived(stop, k):
        send(own.at[k], stop, k, 0, up).wait_recv()

    norm[...] = jnp.zeros_like(norm)

    @pl.loop(0, groups)
    def _(j):
        load(j).wait()
        got = jnp.dot(samples[...], table_v[j], preferred_element_type=F32)
        spec[j] = got
        norm[...] += got[:, :bins] * got[:, :bins] + got[:, bins:] * got[:, bins:]

    power = jnp.sum(norm[...], axis=1, keepdims=True) / (groups * bins)
    norm[...] = jnp.broadcast_to(lax.rsqrt(power + 1e-06), norm.shape)
    for c in range(channels):
        norm[c * segs:(c + 1) * segs, :] *= (1 - bad[c]).astype(F32)

    for k in range(groups):
        real = (spec[k, :, :bins] * norm[...]).reshape(channels, segs, bins)
        imag = (spec[k, :, bins:] * norm[...]).reshape(channels, segs, bins)
        own[k] = jnp.concatenate([real, imag], axis=1).astype(BF16)
        send(own.at[k], 4, k, 0, up).start()

        @pl.when(odd == 0)
        def _():
            send(own.at[k], 2, k, 1, beside).start()

        @pl.when(core == 0)
        def _():
            send(own.at[k], 1, k, 2, sibling).start()

    def exchange(k):
        return pltpu.make_async_remote_copy(
            src_ref=part.at[k],
            dst_ref=peer.at[k],
            send_sem=rep_send.at[k],
            recv_sem=rep_recv.at[k],
            device_id=(blk, other),
            device_id_type=MESH,
        )

    even[...] = jnp.zeros_like(even)
    odd_[...] = jnp.zeros_like(odd_)

    def finish(k):
        exchange(k).wait_recv()
        for side, total in ((0, even), (1, odd_)):
            cross = part[k, side] + peer[k, side]
            high = cross.astype(BF16)
            low = (cross - high.astype(F32)).astype(BF16)
            total[...] += (
                jnp.dot(high, back_v[k, side, 0], preferred_element_type=F32)
                + jnp.dot(low, back_v[k, side, 0], preferred_element_type=F32)
                + jnp.dot(high, back_v[k, side, 1], preferred_element_type=F32)
            )

    back_load.wait()
    for k in range(groups):
        arrived(4, k)

        @pl.when(odd == 1)
        def _():
            send(far[3][k], 2, k, 1, beside).start()

        @pl.when(core == 1)
        def _():
            send(far[3][k], 3, k, 3, sibling).start()

        arrived(2, k)

        @pl.when(core == 1)
        def _():
            send(far[1][k], 1, k, 2, sibling).start()

        @pl.when(core == 0)
        def _():
            send(far[1][k], 3, k, 3, sibling).start()

        arrived(3, k)
        arrived(1, k)

        @pl.loop(0, channels // 4)
        def _(quad):
            for u in range(4):
                g = quad * 4 + u
                mine = own[k, g].astype(F32)
                real_a, imag_a = mine[:segs], mine[segs:]
                for d in range(stops):
                    theirs = far[d][k][offsets[d, g]].astype(F32)
                    real_b, imag_b = theirs[:segs], theirs[segs:]
                    row = pl.ds(d * channels + g, 1)
                    part[k, 0, row, :] = jnp.sum(real_a * real_b + imag_a * imag_b, axis=0, keepdims=True)
                    part[k, 1, row, :] = jnp.sum(imag_a * real_b - real_a * imag_b, axis=0, keepdims=True)

        exchange(k).start()
        if k >= 1:
            finish(k - 1)
    finish(groups - 1)

    corr[...] = ((even[...] - odd_[...]) * scale).reshape(corr.shape)
    flip[...] = ((even[...] + odd_[...]) * scale).reshape(flip.shape)
    back_home = [
        pltpu.make_async_remote_copy(
            src_ref=flip.at[d],
            dst_ref=mirr.at[d],
            send_sem=mir_send.at[d],
            recv_sem=mir_recv.at[d],
            device_id=(lax.rem(blk + n - d - 1, n), rep),
            device_id_type=MESH,
        )
        for d in range(stops)
    ]
    for copy in back_home:
        copy.start()
    for k in range(groups):
        for lane in range(4):
            send(own.at[k], 4, k, lane, up).wait_send()
        exchange(k).wait_send()
    for copy in back_home:
        copy.wait()


def on_device(samples, offsets, bad_mask):
    channels, segs, length = samples.shape
    stops = offsets.shape[0]
    rows = channels * segs
    bins = LANES
    groups = length // 2 // bins
    width = 2 * LAGS + 1
    padded = -(-width // LANES) * LANES
    scale = 1.0 / math.sqrt(segs * lax.axis_size("rep") * (length // 2))
    vmem = pl.BlockSpec(memory_space=pltpu.VMEM)
    smem = pl.BlockSpec(memory_space=pltpu.SMEM)
    hbm = pl.BlockSpec(memory_space=pl.ANY)
    out = jax.ShapeDtypeStruct((stops, channels, padded), F32)
    dma = pltpu.SemaphoreType.DMA
    corr, mirr = pl.pallas_call(
        functools.partial(kernel, scale, groups),
        out_shape=(out, out),
        in_specs=[vmem, hbm, hbm, smem, smem],
        out_specs=(vmem, vmem),
        scratch_shapes=[
            pltpu.VMEM((groups, length, 2 * bins), BF16),
            pltpu.VMEM((groups, 2, 2, bins, padded), BF16),
            pltpu.VMEM((groups, rows, 2 * bins), F32),
            pltpu.VMEM((rows, bins), F32),
            pltpu.VMEM((groups, channels, 2 * segs, bins), BF16),
            pltpu.VMEM((groups, 2, stops * channels, bins), F32),
            pltpu.VMEM((groups, 2, stops * channels, bins), F32),
            pltpu.VMEM((stops * channels, padded), F32),
            pltpu.VMEM((stops * channels, padded), F32),
            pltpu.VMEM((stops, channels, padded), F32),
            dma((groups,)), dma,
            dma((4, groups)), dma((stops, groups)),
            dma((groups,)), dma((groups,)),
            dma((stops,)), dma((stops,)),
        ] + [pltpu.VMEM((channels, 2 * segs, bins), BF16)] * (stops * groups),
        compiler_params=pltpu.CompilerParams(
            collective_id=0, has_side_effects=True, vmem_limit_bytes=48 * 1024 * 1024
        ),
    )(
        samples.reshape(rows, length),
        jnp.asarray(forward_table(length, bins)),
        jnp.asarray(inverse_table(length, LAGS, bins, padded)),
        offsets,
        bad_mask,
    )
    return tuple(jnp.transpose(x, (1, 0, 2))[:, :, :width] for x in (corr, mirr))


def solution(mesh):
    return jax.shard_map(
        on_device,
        mesh=mesh,
        in_specs=(P("blk", "rep", None), P(None, "blk"), P("blk")),
        out_specs=(P("blk", None, None), P("blk", None, None)),
        check_vma=False,
    )
```

```python
import functools
import math

import jax
import jax.numpy as jnp
import ml_dtypes
import numpy as np
from jax import lax
from jax.experimental import pallas as pl
from jax.experimental.pallas import tpu as pltpu
from jax.sharding import PartitionSpec as P

LAGS = 128
LANES = 128
AHEAD = 2
MESH = pl.DeviceIdType.MESH
F32 = jnp.float32
BF16 = jnp.bfloat16


def forward_table(length, bins):
    phase = np.arange(length)[:, None] * np.arange(length // 2)[None, :] % length
    angle = phase * (2.0 * math.pi / length)
    real = np.cos(angle).reshape(length, -1, bins)
    imag = -np.sin(angle).reshape(length, -1, bins)
    both = np.concatenate([real, imag], axis=2).transpose(1, 0, 2)
    return np.ascontiguousarray(both).astype(ml_dtypes.bfloat16)


def inverse_table(length, lag_half, bins, padded):
    width = 2 * lag_half + 1
    lag_idx = np.arange(width) - lag_half
    phase = np.arange(length // 2)[:, None] * (lag_idx[None, :] % length) % length
    angle = phase * (2.0 * math.pi / length)
    whole = np.zeros((2, length // 2, padded), np.float32)
    whole[0, :, :width] = np.cos(angle)
    whole[1, :, :width] = np.sin(angle)
    high = whole.astype(ml_dtypes.bfloat16)
    low = (whole - high.astype(np.float32)).astype(ml_dtypes.bfloat16)
    both = np.stack([high, low], axis=1).reshape(2, 2, -1, bins, padded)
    return np.ascontiguousarray(both.transpose(2, 0, 1, 3, 4))


def kernel(
    scale,
    groups,
    samples_in, table, back, offsets_in, bad_in,
    corr, mirr,
    samples, offsets, bad, in_sem, table_v, back_v, spec, norm, own, part, peer, even, odd_, flip,
    table_sem, back_sem, send_sem, recv_sem, rep_send, rep_recv, mir_send, mir_recv,
    *far_flat,
):
    stops, channels, padded = corr.shape
    rows = samples.shape[0]
    segs = rows // channels
    bins = own.shape[-1]
    far = [far_flat[d * groups:(d + 1) * groups] for d in range(stops)]
    blk, rep = lax.axis_index("blk"), lax.axis_index("rep")
    n = lax.axis_size("blk")
    core = lax.rem(blk, 2)
    odd = lax.rem(blk // 2, 2)
    up = lax.rem(blk + 4, n)
    beside = blk + 2 - 4 * odd
    sibling = blk + 1 - 2 * core
    other = 1 - rep

    def load(j):
        return pltpu.make_async_copy(table.at[j], table_v.at[j], table_sem.at[j])

    small = [
        pltpu.make_async_copy(samples_in, samples, in_sem.at[0]),
        pltpu.make_async_copy(bad_in, bad, in_sem.at[1]),
        pltpu.make_async_copy(offsets_in, offsets, in_sem.at[2]),
    ]
    small[0].start()
    load(0).start()
    small[1].start()
    small[2].start()
    for j in range(1, groups):
        load(j).start()
    back_load = pltpu.make_async_copy(back, back_v, back_sem)
    back_load.start()

    barrier = pltpu.get_barrier_semaphore()
    for by in range(1, stops + 1):
        for who in (lax.rem(blk + by, n), lax.rem(blk + n - by, n)):
            pl.semaphore_signal(barrier, inc=1, device_id=(who, rep), device_id_type=MESH)
    pl.semaphore_signal(barrier, inc=1, device_id=(blk, other), device_id_type=MESH)

    def send(src, stop, k, lane, who):
        return pltpu.make_async_remote_copy(
            src_ref=src,
            dst_ref=far[stop - 1][k],
            send_sem=send_sem.at[lane, k],
            recv_sem=recv_sem.at[stop - 1, k],
            device_id=(who, rep),
            device_id_type=MESH,
        )

    def arrived(stop, k):
        send(own.at[k], stop, k, 0, up).wait_recv()

    norm[...] = jnp.zeros_like(norm)
    small[0].wait()

    @pl.loop(0, groups)
    def _(j):
        load(j).wait()
        got = jnp.dot(samples[...], table_v[j], preferred_element_type=F32)
        spec[j] = got
        norm[...] += got[:, :bins] * got[:, :bins] + got[:, bins:] * got[:, bins:]

    power = jnp.sum(norm[...], axis=1, keepdims=True) / (groups * bins)
    norm[...] = jnp.broadcast_to(lax.rsqrt(power + 1e-06), norm.shape)
    small[1].wait()
    for c in range(channels):
        norm[c * segs:(c + 1) * segs, :] *= (1 - bad[c]).astype(F32)

    pl.semaphore_wait(barrier, 2 * stops + 1)

    def launch(k):
        send(own.at[k], 4, k, 0, up).start()

        @pl.when(odd == 0)
        def _():
            send(own.at[k], 2, k, 1, beside).start()

        @pl.when(core == 0)
        def _():
            send(own.at[k], 1, k, 2, sibling).start()

    for k in range(groups):
        real = (spec[k, :, :bins] * norm[...]).reshape(channels, segs, bins)
        imag = (spec[k, :, bins:] * norm[...]).reshape(channels, segs, bins)
        own[k] = jnp.concatenate([real, imag], axis=1).astype(BF16)
        if k < AHEAD:
            launch(k)

    def exchange(k):
        return pltpu.make_async_remote_copy(
            src_ref=part.at[k],
            dst_ref=peer.at[k],
            send_sem=rep_send.at[k],
            recv_sem=rep_recv.at[k],
            device_id=(blk, other),
            device_id_type=MESH,
        )

    even[...] = jnp.zeros_like(even)
    odd_[...] = jnp.zeros_like(odd_)

    def finish(k):
        exchange(k).wait_recv()
        for side, total in ((0, even), (1, odd_)):
            cross = part[k, side] + peer[k, side]
            high = cross.astype(BF16)
            low = (cross - high.astype(F32)).astype(BF16)
            total[...] += (
                jnp.dot(high, back_v[k, side, 0], preferred_element_type=F32)
                + jnp.dot(low, back_v[k, side, 0], preferred_element_type=F32)
                + jnp.dot(high, back_v[k, side, 1], preferred_element_type=F32)
            )

    back_load.wait()
    small[2].wait()
    for k in range(groups):
        arrived(4, k)
        if k + AHEAD < groups:
            launch(k + AHEAD)

        @pl.when(odd == 1)
        def _():
            send(far[3][k], 2, k, 1, beside).start()

        @pl.when(core == 1)
        def _():
            send(far[3][k], 3, k, 3, sibling).start()

        arrived(2, k)

        @pl.when(core == 1)
        def _():
            send(far[1][k], 1, k, 2, sibling).start()

        @pl.when(core == 0)
        def _():
            send(far[1][k], 3, k, 3, sibling).start()

        arrived(3, k)
        arrived(1, k)

        @pl.loop(0, channels // 4)
        def _(quad):
            for u in range(4):
                g = quad * 4 + u
                mine = own[k, g].astype(F32)
                real_a, imag_a = mine[:segs], mine[segs:]
                for d in range(stops):
                    theirs = far[d][k][offsets[d, g]].astype(F32)
                    real_b, imag_b = theirs[:segs], theirs[segs:]
                    row = pl.ds(d * channels + g, 1)
                    part[k, 0, row, :] = jnp.sum(real_a * real_b + imag_a * imag_b, axis=0, keepdims=True)
                    part[k, 1, row, :] = jnp.sum(imag_a * real_b - real_a * imag_b, axis=0, keepdims=True)

        exchange(k).start()
        if k >= 1:
            finish(k - 1)
    finish(groups - 1)

    corr[...] = ((even[...] - odd_[...]) * scale).reshape(corr.shape)
    flip[...] = ((even[...] + odd_[...]) * scale).reshape(flip.shape)
    back_home = [
        pltpu.make_async_remote_copy(
            src_ref=flip.at[d],
            dst_ref=mirr.at[d],
            send_sem=mir_send.at[d],
            recv_sem=mir_recv.at[d],
            device_id=(lax.rem(blk + n - d - 1, n), rep),
            device_id_type=MESH,
        )
        for d in range(stops)
    ]
    for copy in back_home:
        copy.start()
    for k in range(groups):
        for lane in range(4):
            send(own.at[k], 4, k, lane, up).wait_send()
        exchange(k).wait_send()
    for copy in back_home:
        copy.wait()


def on_device(samples, offsets, bad_mask):
    channels, segs, length = samples.shape
    stops = offsets.shape[0]
    rows = channels * segs
    bins = LANES
    groups = length // 2 // bins
    width = 2 * LAGS + 1
    padded = -(-width // LANES) * LANES
    scale = 1.0 / math.sqrt(segs * lax.axis_size("rep") * (length // 2))
    vmem = pl.BlockSpec(memory_space=pltpu.VMEM)
    hbm = pl.BlockSpec(memory_space=pl.ANY)
    out = jax.ShapeDtypeStruct((stops, channels, padded), F32)
    dma = pltpu.SemaphoreType.DMA
    corr, mirr = pl.pallas_call(
        functools.partial(kernel, scale, groups),
        out_shape=(out, out),
        in_specs=[hbm] * 5,
        out_specs=(vmem, vmem),
        scratch_shapes=[
            pltpu.VMEM((rows, length), BF16),
            pltpu.SMEM((stops, channels), jnp.int32),
            pltpu.SMEM((channels,), jnp.int32),
            dma((3,)),
            pltpu.VMEM((groups, length, 2 * bins), BF16),
            pltpu.VMEM((groups, 2, 2, bins, padded), BF16),
            pltpu.VMEM((groups, rows, 2 * bins), F32),
            pltpu.VMEM((rows, bins), F32),
            pltpu.VMEM((groups, channels, 2 * segs, bins), BF16),
            pltpu.VMEM((groups, 2, stops * channels, bins), F32),
            pltpu.VMEM((groups, 2, stops * channels, bins), F32),
            pltpu.VMEM((stops * channels, padded), F32),
            pltpu.VMEM((stops * channels, padded), F32),
            pltpu.VMEM((stops, channels, padded), F32),
            dma((groups,)), dma,
            dma((4, groups)), dma((stops, groups)),
            dma((groups,)), dma((groups,)),
            dma((stops,)), dma((stops,)),
        ] + [pltpu.VMEM((channels, 2 * segs, bins), BF16)] * (stops * groups),
        compiler_params=pltpu.CompilerParams(
            collective_id=0, has_side_effects=True, vmem_limit_bytes=60 * 1024 * 1024
        ),
    )(
        samples.reshape(rows, length),
        jnp.asarray(forward_table(length, bins)),
        jnp.asarray(inverse_table(length, LAGS, bins, padded)),
        offsets,
        bad_mask,
    )
    return tuple(jnp.transpose(x, (1, 0, 2))[:, :, :width] for x in (corr, mirr))


def solution(mesh):
    return jax.shard_map(
        on_device,
        mesh=mesh,
        in_specs=(P("blk", "rep", None), P(None, "blk"), P("blk")),
        out_specs=(P("blk", None, None), P("blk", None, None)),
        check_vma=False,
    )
```

```python
import functools
import math

import jax
import jax.numpy as jnp
import ml_dtypes
import numpy as np
from jax import lax
from jax.experimental import pallas as pl
from jax.experimental.pallas import tpu as pltpu
from jax.sharding import PartitionSpec as P

LAGS = 128
LANES = 128
AHEAD = 3
SUB = 8
MESH = pl.DeviceIdType.MESH
F32 = jnp.float32
BF16 = jnp.bfloat16


def forward_table(length, bins):
    phase = np.arange(length)[:, None] * np.arange(length // 2)[None, :] % length
    angle = phase * (2.0 * math.pi / length)
    real = np.cos(angle).reshape(length, -1, bins)
    imag = -np.sin(angle).reshape(length, -1, bins)
    both = np.concatenate([real, imag], axis=2).transpose(1, 0, 2)
    return np.ascontiguousarray(both).astype(ml_dtypes.bfloat16)


def inverse_table(length, lag_half, bins, padded):
    width = 2 * lag_half + 1
    lag_idx = np.arange(width) - lag_half
    phase = np.arange(length // 2)[:, None] * (lag_idx[None, :] % length) % length
    angle = phase * (2.0 * math.pi / length)
    whole = np.zeros((2, length // 2, padded), np.float32)
    whole[0, :, :width] = np.cos(angle)
    whole[1, :, :width] = np.sin(angle)
    high = whole.astype(ml_dtypes.bfloat16)
    low = (whole - high.astype(np.float32)).astype(ml_dtypes.bfloat16)
    both = np.stack([high, low], axis=1).reshape(2, 2, -1, bins, padded)
    return np.ascontiguousarray(both.transpose(2, 0, 1, 3, 4))


def sum_rows(tiles):
    row = lax.broadcasted_iota(jnp.int32, tiles[0].shape, 0)
    low = row < 4
    tiles = [
        jnp.where(low, tiles[i], tiles[i + 4]) + pltpu.roll(jnp.where(low, tiles[i + 4], tiles[i]), 4, 0)
        for i in range(4)
    ]
    low = lax.rem(row, 4) < 2
    tiles = [
        jnp.where(low, tiles[i] + pltpu.roll(tiles[i], 6, 0), tiles[i + 2] + pltpu.roll(tiles[i + 2], 2, 0))
        for i in range(2)
    ]
    low = lax.rem(row, 2) < 1
    return jnp.where(low, tiles[0] + pltpu.roll(tiles[0], 7, 0), tiles[1] + pltpu.roll(tiles[1], 1, 0))


def kernel(
    scale,
    groups,
    samples_in, table, back, offsets_in, bad_in,
    corr, mirr,
    samples, offsets, bad, in_sem, table_v, back_v, spec, norm, own, part, peer, even, odd_, flip,
    table_sem, back_sem, send_sem, recv_sem, rep_send, rep_recv, mir_send, mir_recv,
    *far_flat,
):
    stops, channels, padded = corr.shape
    rows = samples.shape[0]
    segs = rows // channels
    bins = own.shape[-1]
    far = [far_flat[d * groups:(d + 1) * groups] for d in range(stops)]
    blk, rep = lax.axis_index("blk"), lax.axis_index("rep")
    n = lax.axis_size("blk")
    core = lax.rem(blk, 2)
    odd = lax.rem(blk // 2, 2)
    up = lax.rem(blk + 4, n)
    beside = blk + 2 - 4 * odd
    sibling = blk + 1 - 2 * core
    other = 1 - rep

    def load(j):
        return pltpu.make_async_copy(table.at[j], table_v.at[j], table_sem.at[j])

    small = [
        pltpu.make_async_copy(samples_in, samples, in_sem.at[0]),
        pltpu.make_async_copy(bad_in, bad, in_sem.at[1]),
        pltpu.make_async_copy(offsets_in, offsets, in_sem.at[2]),
    ]
    small[0].start()
    load(0).start()
    small[1].start()
    small[2].start()
    for j in range(1, groups):
        load(j).start()
    back_load = pltpu.make_async_copy(back, back_v, back_sem)
    back_load.start()

    barrier = pltpu.get_barrier_semaphore()
    for by in range(1, stops + 1):
        for who in (lax.rem(blk + by, n), lax.rem(blk + n - by, n)):
            pl.semaphore_signal(barrier, inc=1, device_id=(who, rep), device_id_type=MESH)
    pl.semaphore_signal(barrier, inc=1, device_id=(blk, other), device_id_type=MESH)

    def send(src, stop, k, lane, who):
        return pltpu.make_async_remote_copy(
            src_ref=src,
            dst_ref=far[stop - 1][k],
            send_sem=send_sem.at[lane, k],
            recv_sem=recv_sem.at[stop - 1, k],
            device_id=(who, rep),
            device_id_type=MESH,
        )

    def arrived(stop, k):
        send(own.at[k], stop, k, 0, up).wait_recv()

    norm[...] = jnp.zeros_like(norm)
    small[0].wait()

    @pl.loop(0, groups)
    def _(j):
        load(j).wait()
        got = jnp.dot(samples[...], table_v[j], preferred_element_type=F32)
        spec[j] = got
        norm[...] += got[:, :bins] * got[:, :bins] + got[:, bins:] * got[:, bins:]

    power = jnp.sum(norm[...], axis=1, keepdims=True) / (groups * bins)
    norm[...] = jnp.broadcast_to(lax.rsqrt(power + 1e-06), norm.shape)
    small[1].wait()
    for c in range(channels):
        norm[c * segs:(c + 1) * segs, :] *= (1 - bad[c]).astype(F32)

    pl.semaphore_wait(barrier, 2 * stops + 1)

    def launch(k):
        send(own.at[k], 4, k, 0, up).start()

        @pl.when(odd == 0)
        def _():
            send(own.at[k], 2, k, 1, beside).start()

        @pl.when(core == 0)
        def _():
            send(own.at[k], 1, k, 2, sibling).start()

    for k in range(groups):
        real = (spec[k, :, :bins] * norm[...]).reshape(channels, segs, bins)
        imag = (spec[k, :, bins:] * norm[...]).reshape(channels, segs, bins)
        own[k] = jnp.concatenate([real, imag], axis=1).astype(BF16)
        if k < AHEAD:
            launch(k)

    def exchange(k):
        return pltpu.make_async_remote_copy(
            src_ref=part.at[k],
            dst_ref=peer.at[k],
            send_sem=rep_send.at[k],
            recv_sem=rep_recv.at[k],
            device_id=(blk, other),
            device_id_type=MESH,
        )

    even[...] = jnp.zeros_like(even)
    odd_[...] = jnp.zeros_like(odd_)

    def finish(pair):
        first, second = 2 * pair, 2 * pair + 1
        exchange(first).wait_recv()
        exchange(second).wait_recv()
        for side, total in ((0, even), (1, odd_)):
            cross = jnp.concatenate([part[k, side] + peer[k, side] for k in (first, second)], axis=1)
            high = cross.astype(BF16)
            low = (cross - high.astype(F32)).astype(BF16)
            total[...] += (
                jnp.dot(high, back_v[pair, side, 0], preferred_element_type=F32)
                + jnp.dot(low, back_v[pair, side, 0], preferred_element_type=F32)
                + jnp.dot(high, back_v[pair, side, 1], preferred_element_type=F32)
            )

    back_load.wait()
    small[2].wait()
    for k in range(groups):
        arrived(4, k)
        if k + AHEAD < groups:
            launch(k + AHEAD)

        @pl.when(odd == 1)
        def _():
            send(far[3][k], 2, k, 1, beside).start()

        @pl.when(core == 1)
        def _():
            send(far[3][k], 3, k, 3, sibling).start()

        arrived(2, k)

        @pl.when(core == 1)
        def _():
            send(far[1][k], 1, k, 2, sibling).start()

        @pl.when(core == 0)
        def _():
            send(far[1][k], 3, k, 3, sibling).start()

        arrived(3, k)
        arrived(1, k)

        @pl.loop(0, channels // SUB)
        def _(octet):
            base = octet * SUB
            for d in range(stops):
                reals, imags = [], []
                for u in range(SUB):
                    mine = own[k, base + u].astype(F32)
                    theirs = far[d][k][offsets[d, base + u]].astype(F32)
                    real_a, imag_a = mine[:segs], mine[segs:]
                    real_b, imag_b = theirs[:segs], theirs[segs:]
                    reals.append(real_a * real_b + imag_a * imag_b)
                    imags.append(imag_a * real_b - real_a * imag_b)
                place = pl.ds(pl.multiple_of(d * channels + base, SUB), SUB)
                part[k, 0, place, :] = sum_rows(reals)
                part[k, 1, place, :] = sum_rows(imags)

        exchange(k).start()
        if k >= 2 and k % 2 == 0:
            finish(k // 2 - 1)
    finish(groups // 2 - 1)

    corr[...] = ((even[...] - odd_[...]) * scale).reshape(corr.shape)
    flip[...] = ((even[...] + odd_[...]) * scale).reshape(flip.shape)
    back_home = [
        pltpu.make_async_remote_copy(
            src_ref=flip.at[d],
            dst_ref=mirr.at[d],
            send_sem=mir_send.at[d],
            recv_sem=mir_recv.at[d],
            device_id=(lax.rem(blk + n - d - 1, n), rep),
            device_id_type=MESH,
        )
        for d in range(stops)
    ]
    for copy in back_home:
        copy.start()
    for k in range(groups):
        for lane in range(4):
            send(own.at[k], 4, k, lane, up).wait_send()
        exchange(k).wait_send()
    for copy in back_home:
        copy.wait()


def on_device(samples, offsets, bad_mask):
    channels, segs, length = samples.shape
    stops = offsets.shape[0]
    rows = channels * segs
    bins = LANES
    assert segs == SUB and channels % SUB == 0
    groups = length // 2 // bins
    width = 2 * LAGS + 1
    padded = -(-width // LANES) * LANES
    scale = 1.0 / math.sqrt(segs * lax.axis_size("rep") * (length // 2))
    vmem = pl.BlockSpec(memory_space=pltpu.VMEM)
    hbm = pl.BlockSpec(memory_space=pl.ANY)
    out = pltpu.VMEM((stops, channels, padded), F32)
    dma = pltpu.SemaphoreType.DMA
    corr, mirr = pl.pallas_call(
        functools.partial(kernel, scale, groups),
        out_shape=(out, out),
        in_specs=[hbm] * 5,
        out_specs=(vmem, vmem),
        scratch_shapes=[
            pltpu.VMEM((rows, length), BF16),
            pltpu.SMEM((stops, channels), jnp.int32),
            pltpu.SMEM((channels,), jnp.int32),
            dma((3,)),
            pltpu.VMEM((groups, length, 2 * bins), BF16),
            pltpu.VMEM((groups // 2, 2, 2, 2 * bins, padded), BF16),
            pltpu.VMEM((groups, rows, 2 * bins), F32),
            pltpu.VMEM((rows, bins), F32),
            pltpu.VMEM((groups, channels, 2 * segs, bins), BF16),
            pltpu.VMEM((groups, 2, stops * channels, bins), F32),
            pltpu.VMEM((groups, 2, stops * channels, bins), F32),
            pltpu.VMEM((stops * channels, padded), F32),
            pltpu.VMEM((stops * channels, padded), F32),
            pltpu.VMEM((stops, channels, padded), F32),
            dma((groups,)), dma,
            dma((4, groups)), dma((stops, groups)),
            dma((groups,)), dma((groups,)),
            dma((stops,)), dma((stops,)),
        ] + [pltpu.VMEM((channels, 2 * segs, bins), BF16)] * (stops * groups),
        compiler_params=pltpu.CompilerParams(
            collective_id=0, has_side_effects=True, vmem_limit_bytes=57 * 1024 * 1024
        ),
    )(
        samples.reshape(rows, length),
        jnp.asarray(forward_table(length, bins)),
        jnp.asarray(inverse_table(length, LAGS, 2 * bins, padded)),
        offsets,
        bad_mask,
    )
    return tuple(jnp.transpose(x, (1, 0, 2))[:, :, :width] for x in (corr, mirr))


def solution(mesh):
    return jax.shard_map(
        on_device,
        mesh=mesh,
        in_specs=(P("blk", "rep", None), P(None, "blk"), P("blk")),
        out_specs=(P("blk", None, None), P("blk", None, None)),
        check_vma=False,
    )
```

```python
import functools
import math

import jax
import jax.numpy as jnp
import ml_dtypes
import numpy as np
from jax import lax
from jax.experimental import pallas as pl
from jax.experimental.pallas import tpu as pltpu
from jax.sharding import PartitionSpec as P

LAGS = 128
LANES = 128
AHEAD = 3
SUB = 8
PIECES = 4
MESH = pl.DeviceIdType.MESH
F32 = jnp.float32
BF16 = jnp.bfloat16


def forward_table(length, bins):
    phase = np.arange(length)[:, None] * np.arange(length // 2)[None, :] % length
    angle = phase * (2.0 * math.pi / length)
    real = np.cos(angle).reshape(length, -1, bins)
    imag = -np.sin(angle).reshape(length, -1, bins)
    both = np.concatenate([real, imag], axis=2).transpose(1, 0, 2)
    return np.ascontiguousarray(both).astype(ml_dtypes.bfloat16)


def inverse_table(length, lag_half, bins, padded):
    width = 2 * lag_half + 1
    lag_idx = np.arange(width) - lag_half
    phase = np.arange(length // 2)[:, None] * (lag_idx[None, :] % length) % length
    angle = phase * (2.0 * math.pi / length)
    whole = np.zeros((2, length // 2, padded), np.float32)
    whole[0, :, :width] = np.cos(angle)
    whole[1, :, :width] = np.sin(angle)
    high = whole.astype(ml_dtypes.bfloat16)
    low = (whole - high.astype(np.float32)).astype(ml_dtypes.bfloat16)
    both = np.stack([high, low], axis=1).reshape(2, 2, -1, bins, padded)
    return np.ascontiguousarray(both.transpose(2, 0, 1, 3, 4))


def sum_rows(tiles):
    row = lax.broadcasted_iota(jnp.int32, tiles[0].shape, 0)
    low = row < 4
    tiles = [
        jnp.where(low, tiles[i], tiles[i + 4]) + pltpu.roll(jnp.where(low, tiles[i + 4], tiles[i]), 4, 0)
        for i in range(4)
    ]
    low = lax.rem(row, 4) < 2
    tiles = [
        jnp.where(low, tiles[i] + pltpu.roll(tiles[i], 6, 0), tiles[i + 2] + pltpu.roll(tiles[i + 2], 2, 0))
        for i in range(2)
    ]
    low = lax.rem(row, 2) < 1
    return jnp.where(low, tiles[0] + pltpu.roll(tiles[0], 7, 0), tiles[1] + pltpu.roll(tiles[1], 1, 0))


def kernel(
    scale,
    groups,
    samples_in, table, back, offsets_in, bad_in,
    corr, mirr,
    samples, offsets, bad, in_sem, table_v, back_v, spec, norm, own, part, peer, even, odd_, flip,
    table_sem, back_sem, send_sem, recv_sem, rep_send, rep_recv, mir_send, mir_recv,
    *far_flat,
):
    stops, channels, padded = corr.shape
    rows = samples.shape[0]
    segs = rows // channels
    bins = own.shape[-1]
    far = [far_flat[d * groups:(d + 1) * groups] for d in range(stops)]
    blk, rep = lax.axis_index("blk"), lax.axis_index("rep")
    n = lax.axis_size("blk")
    core = lax.rem(blk, 2)
    odd = lax.rem(blk // 2, 2)
    up = lax.rem(blk + 4, n)
    beside = blk + 2 - 4 * odd
    sibling = blk + 1 - 2 * core
    other = 1 - rep

    def load(j):
        return pltpu.make_async_copy(table.at[j], table_v.at[j], table_sem.at[j])

    small = [
        pltpu.make_async_copy(samples_in, samples, in_sem.at[0]),
        pltpu.make_async_copy(bad_in, bad, in_sem.at[1]),
        pltpu.make_async_copy(offsets_in, offsets, in_sem.at[2]),
    ]
    small[0].start()
    load(0).start()
    small[1].start()
    small[2].start()
    for j in range(1, groups):
        load(j).start()
    back_load = pltpu.make_async_copy(back, back_v, back_sem)
    back_load.start()

    barrier = pltpu.get_barrier_semaphore()
    for by in range(1, stops + 1):
        for who in (lax.rem(blk + by, n), lax.rem(blk + n - by, n)):
            pl.semaphore_signal(barrier, inc=1, device_id=(who, rep), device_id_type=MESH)
    pl.semaphore_signal(barrier, inc=1, device_id=(blk, other), device_id_type=MESH)

    def pieces(k):
        return PIECES if k == groups - 1 else 1

    def send(src, stop, k, lane, who, piece=None):
        dst = far[stop - 1][k]
        if piece is not None and pieces(k) > 1:
            size = channels // PIECES
            src, dst = (ref.at[pl.ds(piece * size, size)] for ref in (src, dst))
        return pltpu.make_async_remote_copy(
            src_ref=src,
            dst_ref=dst,
            send_sem=send_sem.at[lane, k, piece or 0],
            recv_sem=recv_sem.at[stop - 1, k, piece or 0],
            device_id=(who, rep),
            device_id_type=MESH,
        )

    def arrived(stop, k, piece=None):
        send(own.at[k], stop, k, 0, up, piece).wait_recv()

    norm[...] = jnp.zeros_like(norm)
    small[0].wait()

    @pl.loop(0, groups)
    def _(j):
        load(j).wait()
        got = jnp.dot(samples[...], table_v[j], preferred_element_type=F32)
        spec[j] = got
        norm[...] += got[:, :bins] * got[:, :bins] + got[:, bins:] * got[:, bins:]

    power = jnp.sum(norm[...], axis=1, keepdims=True) / (groups * bins)
    norm[...] = jnp.broadcast_to(lax.rsqrt(power + 1e-06), norm.shape)
    small[1].wait()
    for c in range(channels):
        norm[c * segs:(c + 1) * segs, :] *= (1 - bad[c]).astype(F32)

    pl.semaphore_wait(barrier, 2 * stops + 1)

    def launch(k):
        for piece in range(pieces(k)):
            send(own.at[k], 4, k, 0, up, piece).start()

            @pl.when(odd == 0)
            def _():
                send(own.at[k], 2, k, 1, beside, piece).start()

        @pl.when(core == 0)
        def _():
            send(own.at[k], 1, k, 2, sibling).start()

    for k in range(groups):
        real = (spec[k, :, :bins] * norm[...]).reshape(channels, segs, bins)
        imag = (spec[k, :, bins:] * norm[...]).reshape(channels, segs, bins)
        own[k] = jnp.concatenate([real, imag], axis=1).astype(BF16)
        if k < AHEAD:
            launch(k)

    def exchange(k, d):
        return pltpu.make_async_remote_copy(
            src_ref=part.at[k, d],
            dst_ref=peer.at[k, d],
            send_sem=rep_send.at[k, d],
            recv_sem=rep_recv.at[k, d],
            device_id=(blk, other),
            device_id_type=MESH,
        )

    def pair_up(k, stop):
        d = stop - 1

        @pl.loop(0, channels // SUB)
        def _(octet):
            base = pl.multiple_of(octet * SUB, SUB)
            reals, imags = [], []
            for u in range(SUB):
                mine = own[k, base + u].astype(F32)
                theirs = far[d][k][offsets[d, base + u]].astype(F32)
                real_a, imag_a = mine[:segs], mine[segs:]
                real_b, imag_b = theirs[:segs], theirs[segs:]
                reals.append(real_a * real_b + imag_a * imag_b)
                imags.append(imag_a * real_b - real_a * imag_b)
            part[k, d, 0, pl.ds(base, SUB), :] = sum_rows(reals)
            part[k, d, 1, pl.ds(base, SUB), :] = sum_rows(imags)

        exchange(k, d).start()

    even[...] = jnp.zeros_like(even)
    odd_[...] = jnp.zeros_like(odd_)

    def finish(pair):
        first, second = 2 * pair, 2 * pair + 1
        for d in range(stops):
            exchange(first, d).wait_recv()
            exchange(second, d).wait_recv()
        for side, total in ((0, even), (1, odd_)):
            cross = jnp.concatenate(
                [(part[k, :, side] + peer[k, :, side]).reshape(stops * channels, bins) for k in (first, second)], axis=1
            )
            high = cross.astype(BF16)
            low = (cross - high.astype(F32)).astype(BF16)
            total[...] += (
                jnp.dot(high, back_v[pair, side, 0], preferred_element_type=F32)
                + jnp.dot(low, back_v[pair, side, 0], preferred_element_type=F32)
                + jnp.dot(high, back_v[pair, side, 1], preferred_element_type=F32)
            )

    back_load.wait()
    small[2].wait()
    for k in range(groups):
        for piece in range(pieces(k)):
            arrived(4, k, piece)

            @pl.when(odd == 1)
            def _():
                send(far[3][k], 2, k, 1, beside, piece).start()

        @pl.when(core == 1)
        def _():
            send(far[3][k], 3, k, 3, sibling).start()

        if k + AHEAD < groups:
            launch(k + AHEAD)
        pair_up(k, 4)
        for piece in range(pieces(k)):
            arrived(2, k, piece)

        @pl.when(core == 1)
        def _():
            send(far[1][k], 1, k, 2, sibling).start()

        @pl.when(core == 0)
        def _():
            send(far[1][k], 3, k, 3, sibling).start()

        pair_up(k, 2)
        for stop in (3, 1):
            arrived(stop, k)
            pair_up(k, stop)
        if k >= 2 and k % 2 == 0:
            finish(k // 2 - 1)
    finish(groups // 2 - 1)

    flip[...] = ((even[...] + odd_[...]) * scale).reshape(flip.shape)
    back_home = [
        pltpu.make_async_remote_copy(
            src_ref=flip.at[d],
            dst_ref=mirr.at[d],
            send_sem=mir_send.at[d],
            recv_sem=mir_recv.at[d],
            device_id=(lax.rem(blk + n - d - 1, n), rep),
            device_id_type=MESH,
        )
        for d in range(stops)
    ]
    for copy in back_home:
        copy.start()
    corr[...] = ((even[...] - odd_[...]) * scale).reshape(corr.shape)
    for k in range(groups):
        for lane in range(4):
            for piece in range(pieces(k) if lane < 2 else 1):
                send(own.at[k], 4, k, lane, up, piece if lane < 2 else None).wait_send()
        for d in range(stops):
            exchange(k, d).wait_send()
    for copy in back_home:
        copy.wait()


def on_device(samples, offsets, bad_mask):
    channels, segs, length = samples.shape
    stops = offsets.shape[0]
    rows = channels * segs
    bins = LANES
    assert segs == SUB and channels % SUB == 0
    groups = length // 2 // bins
    width = 2 * LAGS + 1
    padded = -(-width // LANES) * LANES
    scale = 1.0 / math.sqrt(segs * lax.axis_size("rep") * (length // 2))
    vmem = pl.BlockSpec(memory_space=pltpu.VMEM)
    hbm = pl.BlockSpec(memory_space=pl.ANY)
    out = pltpu.VMEM((stops, channels, padded), F32)
    dma = pltpu.SemaphoreType.DMA
    corr, mirr = pl.pallas_call(
        functools.partial(kernel, scale, groups),
        out_shape=(out, out),
        in_specs=[hbm] * 5,
        out_specs=(vmem, vmem),
        scratch_shapes=[
            pltpu.VMEM((rows, length), BF16),
            pltpu.SMEM((stops, channels), jnp.int32),
            pltpu.SMEM((channels,), jnp.int32),
            dma((3,)),
            pltpu.VMEM((groups, length, 2 * bins), BF16),
            pltpu.VMEM((groups // 2, 2, 2, 2 * bins, padded), BF16),
            pltpu.VMEM((groups, rows, 2 * bins), F32),
            pltpu.VMEM((rows, bins), F32),
            pltpu.VMEM((groups, channels, 2 * segs, bins), BF16),
            pltpu.VMEM((groups, stops, 2, channels, bins), F32),
            pltpu.VMEM((groups, stops, 2, channels, bins), F32),
            pltpu.VMEM((stops * channels, padded), F32),
            pltpu.VMEM((stops * channels, padded), F32),
            pltpu.VMEM((stops, channels, padded), F32),
            dma((groups,)), dma,
            dma((4, groups, PIECES)), dma((stops, groups, PIECES)),
            dma((groups, stops)), dma((groups, stops)),
            dma((stops,)), dma((stops,)),
        ] + [pltpu.VMEM((channels, 2 * segs, bins), BF16)] * (stops * groups),
        compiler_params=pltpu.CompilerParams(
            collective_id=0, has_side_effects=True, vmem_limit_bytes=57 * 1024 * 1024
        ),
    )(
        samples.reshape(rows, length),
        jnp.asarray(forward_table(length, bins)),
        jnp.asarray(inverse_table(length, LAGS, 2 * bins, padded)),
        offsets,
        bad_mask,
    )
    return tuple(jnp.transpose(x, (1, 0, 2))[:, :, :width] for x in (corr, mirr))


def solution(mesh):
    return jax.shard_map(
        on_device,
        mesh=mesh,
        in_specs=(P("blk", "rep", None), P(None, "blk"), P("blk")),
        out_specs=(P("blk", None, None), P("blk", None, None)),
        check_vma=False,
    )
```

```python
import functools
import math

import jax
import jax.numpy as jnp
import ml_dtypes
import numpy as np
from jax import lax
from jax.experimental import pallas as pl
from jax.experimental.pallas import tpu as pltpu
from jax.sharding import PartitionSpec as P

LAGS = 128
LANES = 128
AHEAD = 3
SUB = 8
PIECES = 4
MESH = pl.DeviceIdType.MESH
F32 = jnp.float32
BF16 = jnp.bfloat16


def forward_table(length, bins):
    phase = np.arange(length)[:, None] * np.arange(length // 2)[None, :] % length
    angle = phase * (2.0 * math.pi / length)
    real = np.cos(angle).reshape(length, -1, bins)
    imag = -np.sin(angle).reshape(length, -1, bins)
    both = np.concatenate([real, imag], axis=2).transpose(1, 0, 2)
    return np.ascontiguousarray(both).astype(ml_dtypes.bfloat16)


def inverse_table(length, lag_half, bins, padded):
    width = 2 * lag_half + 1
    lag_idx = np.arange(width) - lag_half
    phase = np.arange(length // 2)[:, None] * (lag_idx[None, :] % length) % length
    angle = phase * (2.0 * math.pi / length)
    whole = np.zeros((2, length // 2, padded), np.float32)
    whole[0, :, :width] = np.cos(angle)
    whole[1, :, :width] = np.sin(angle)
    high = whole.astype(ml_dtypes.bfloat16)
    low = (whole - high.astype(np.float32)).astype(ml_dtypes.bfloat16)
    both = np.stack([high, low], axis=1).reshape(2, 2, -1, bins, padded)
    return np.ascontiguousarray(both.transpose(2, 0, 1, 3, 4))


def sum_rows(tiles):
    row = lax.broadcasted_iota(jnp.int32, tiles[0].shape, 0)
    low = row < 4
    tiles = [
        jnp.where(low, tiles[i], tiles[i + 4]) + pltpu.roll(jnp.where(low, tiles[i + 4], tiles[i]), 4, 0)
        for i in range(4)
    ]
    low = lax.rem(row, 4) < 2
    tiles = [
        jnp.where(low, tiles[i] + pltpu.roll(tiles[i], 6, 0), tiles[i + 2] + pltpu.roll(tiles[i + 2], 2, 0))
        for i in range(2)
    ]
    low = lax.rem(row, 2) < 1
    return jnp.where(low, tiles[0] + pltpu.roll(tiles[0], 7, 0), tiles[1] + pltpu.roll(tiles[1], 1, 0))


def kernel(
    scale,
    groups,
    samples_in, table, back, offsets_in, bad_in,
    corr, mirr,
    samples, offsets, bad, in_sem, table_v, back_v, spec, norm, own, part, peer, even, odd_, flip,
    table_sem, back_sem, send_sem, recv_sem, rep_send, rep_recv, mir_send, mir_recv,
    *far_flat,
):
    stops, channels, padded = corr.shape
    rows = samples.shape[0]
    segs = rows // channels
    bins = own.shape[-1]
    far = [far_flat[d * groups:(d + 1) * groups] for d in range(stops)]
    blk, rep = lax.axis_index("blk"), lax.axis_index("rep")
    n = lax.axis_size("blk")
    core = lax.rem(blk, 2)
    odd = lax.rem(blk // 2, 2)
    up = lax.rem(blk + 4, n)
    beside = blk + 2 - 4 * odd
    sibling = blk + 1 - 2 * core
    other = 1 - rep

    def load(j):
        return pltpu.make_async_copy(table.at[j], table_v.at[j], table_sem.at[j])

    small = [
        pltpu.make_async_copy(samples_in, samples, in_sem.at[0]),
        pltpu.make_async_copy(bad_in, bad, in_sem.at[1]),
        pltpu.make_async_copy(offsets_in, offsets, in_sem.at[2]),
    ]
    small[0].start()
    load(0).start()
    small[1].start()
    small[2].start()
    for j in range(1, groups):
        load(j).start()
    back_load = pltpu.make_async_copy(back, back_v, back_sem)

    barrier = pltpu.get_barrier_semaphore()
    for by in range(1, stops + 1):
        for who in (lax.rem(blk + by, n), lax.rem(blk + n - by, n)):
            pl.semaphore_signal(barrier, inc=1, device_id=(who, rep), device_id_type=MESH)
    pl.semaphore_signal(barrier, inc=1, device_id=(blk, other), device_id_type=MESH)

    def pieces(k):
        return PIECES if k == groups - 1 else 1

    def send(src, stop, k, lane, who, piece=None):
        dst = far[stop - 1][k]
        if piece is not None and pieces(k) > 1:
            size = channels // PIECES
            src, dst = (ref.at[pl.ds(piece * size, size)] for ref in (src, dst))
        return pltpu.make_async_remote_copy(
            src_ref=src,
            dst_ref=dst,
            send_sem=send_sem.at[lane, k, piece or 0],
            recv_sem=recv_sem.at[stop - 1, k, piece or 0],
            device_id=(who, rep),
            device_id_type=MESH,
        )

    def arrived(stop, k, piece=None):
        send(own.at[k], stop, k, 0, up, piece).wait_recv()

    norm[...] = jnp.zeros_like(norm)
    small[0].wait()

    @pl.loop(0, groups)
    def _(j):
        load(j).wait()
        got = jnp.dot(samples[...], table_v[j], preferred_element_type=F32)
        spec[j] = got
        norm[...] += got[:, :bins] * got[:, :bins] + got[:, bins:] * got[:, bins:]

    back_load.start()
    power = jnp.sum(norm[...], axis=1, keepdims=True) / (groups * bins)
    norm[...] = jnp.broadcast_to(lax.rsqrt(power + 1e-06), norm.shape)
    small[1].wait()
    for c in range(channels):
        norm[c * segs:(c + 1) * segs, :] *= (1 - bad[c]).astype(F32)

    pl.semaphore_wait(barrier, 2 * stops + 1)

    def launch(k):
        for piece in range(pieces(k)):
            send(own.at[k], 4, k, 0, up, piece).start()

            @pl.when(odd == 0)
            def _():
                send(own.at[k], 2, k, 1, beside, piece).start()

        @pl.when(core == 0)
        def _():
            send(own.at[k], 1, k, 2, sibling).start()

    for k in range(groups):
        real = (spec[k, :, :bins] * norm[...]).reshape(channels, segs, bins)
        imag = (spec[k, :, bins:] * norm[...]).reshape(channels, segs, bins)
        own[k] = jnp.concatenate([real, imag], axis=1).astype(BF16)
        if k < AHEAD:
            launch(k)

    def exchange(k, d):
        return pltpu.make_async_remote_copy(
            src_ref=part.at[k, d],
            dst_ref=peer.at[k, d],
            send_sem=rep_send.at[k, d],
            recv_sem=rep_recv.at[k, d],
            device_id=(blk, other),
            device_id_type=MESH,
        )

    def pair_up(k, stop):
        d = stop - 1

        @pl.loop(0, channels // SUB)
        def _(octet):
            base = pl.multiple_of(octet * SUB, SUB)
            reals, imags = [], []
            for u in range(SUB):
                mine = own[k, base + u].astype(F32)
                theirs = far[d][k][offsets[d, base + u]].astype(F32)
                real_a, imag_a = mine[:segs], mine[segs:]
                real_b, imag_b = theirs[:segs], theirs[segs:]
                reals.append(real_a * real_b + imag_a * imag_b)
                imags.append(imag_a * real_b - real_a * imag_b)
            part[k, d, 0, pl.ds(base, SUB), :] = sum_rows(reals)
            part[k, d, 1, pl.ds(base, SUB), :] = sum_rows(imags)

        exchange(k, d).start()

    even[...] = jnp.zeros_like(even)
    odd_[...] = jnp.zeros_like(odd_)

    def finish(pair, stops_done):
        first, second = 2 * pair, 2 * pair + 1
        low_d, high_d = min(stops_done) - 1, max(stops_done)
        for d in range(low_d, high_d):
            exchange(first, d).wait_recv()
            exchange(second, d).wait_recv()
        count = (high_d - low_d) * channels
        held = pl.ds(low_d * channels, count)
        for side, total in ((0, even), (1, odd_)):
            cross = jnp.concatenate(
                [
                    (part[k, low_d:high_d, side] + peer[k, low_d:high_d, side]).reshape(count, bins)
                    for k in (first, second)
                ],
                axis=1,
            )
            high = cross.astype(BF16)
            low = (cross - high.astype(F32)).astype(BF16)
            total[held, :] += (
                jnp.dot(high, back_v[pair, side, 0], preferred_element_type=F32)
                + jnp.dot(low, back_v[pair, side, 0], preferred_element_type=F32)
                + jnp.dot(high, back_v[pair, side, 1], preferred_element_type=F32)
            )

    def go_home(d):
        return pltpu.make_async_remote_copy(
            src_ref=flip.at[d],
            dst_ref=mirr.at[d],
            send_sem=mir_send.at[d],
            recv_sem=mir_recv.at[d],
            device_id=(lax.rem(blk + n - d - 1, n), rep),
            device_id_type=MESH,
        )

    def conclude(stop):
        d = stop - 1
        finish(groups // 2 - 1, (stop,))
        held = pl.ds(d * channels, channels)
        flip[d] = (even[held, :] + odd_[held, :]) * scale
        go_home(d).start()
        corr[d] = (even[held, :] - odd_[held, :]) * scale

    back_load.wait()
    small[2].wait()
    for k in range(groups):
        for piece in range(pieces(k)):
            arrived(4, k, piece)

            @pl.when(odd == 1)
            def _():
                send(far[3][k], 2, k, 1, beside, piece).start()

        @pl.when(core == 1)
        def _():
            send(far[3][k], 3, k, 3, sibling).start()

        if k + AHEAD < groups:
            launch(k + AHEAD)
        pair_up(k, 4)
        for piece in range(pieces(k)):
            arrived(2, k, piece)

        @pl.when(core == 1)
        def _():
            send(far[1][k], 1, k, 2, sibling).start()

        @pl.when(core == 0)
        def _():
            send(far[1][k], 3, k, 3, sibling).start()

        pair_up(k, 2)
        for stop in (3, 1):
            arrived(stop, k)
            pair_up(k, stop)
            if k == groups - 1:
                conclude(4 if stop == 3 else 2)
        if k >= 2 and k % 2 == 0:
            finish(k // 2 - 1, range(1, stops + 1))
    conclude(3)
    conclude(1)
    for k in range(groups):
        for lane in range(4):
            for piece in range(pieces(k) if lane < 2 else 1):
                send(own.at[k], 4, k, lane, up, piece if lane < 2 else None).wait_send()
        for d in range(stops):
            exchange(k, d).wait_send()
    for d in range(stops):
        go_home(d).wait()


def on_device(samples, offsets, bad_mask):
    channels, segs, length = samples.shape
    stops = offsets.shape[0]
    rows = channels * segs
    bins = LANES
    assert segs == SUB and channels % SUB == 0
    groups = length // 2 // bins
    width = 2 * LAGS + 1
    padded = -(-width // LANES) * LANES
    scale = 1.0 / math.sqrt(segs * lax.axis_size("rep") * (length // 2))
    vmem = pl.BlockSpec(memory_space=pltpu.VMEM)
    hbm = pl.BlockSpec(memory_space=pl.ANY)
    out = pltpu.VMEM((stops, channels, padded), F32)
    dma = pltpu.SemaphoreType.DMA
    corr, mirr = pl.pallas_call(
        functools.partial(kernel, scale, groups),
        out_shape=(out, out),
        in_specs=[hbm] * 5,
        out_specs=(vmem, vmem),
        scratch_shapes=[
            pltpu.VMEM((rows, length), BF16),
            pltpu.SMEM((stops, channels), jnp.int32),
            pltpu.SMEM((channels,), jnp.int32),
            dma((3,)),
            pltpu.VMEM((groups, length, 2 * bins), BF16),
            pltpu.VMEM((groups // 2, 2, 2, 2 * bins, padded), BF16),
            pltpu.VMEM((groups, rows, 2 * bins), F32),
            pltpu.VMEM((rows, bins), F32),
            pltpu.VMEM((groups, channels, 2 * segs, bins), BF16),
            pltpu.VMEM((groups, stops, 2, channels, bins), F32),
            pltpu.VMEM((groups, stops, 2, channels, bins), F32),
            pltpu.VMEM((stops * channels, padded), F32),
            pltpu.VMEM((stops * channels, padded), F32),
            pltpu.VMEM((stops, channels, padded), F32),
            dma((groups,)), dma,
            dma((4, groups, PIECES)), dma((stops, groups, PIECES)),
            dma((groups, stops)), dma((groups, stops)),
            dma((stops,)), dma((stops,)),
        ] + [pltpu.VMEM((channels, 2 * segs, bins), BF16)] * (stops * groups),
        compiler_params=pltpu.CompilerParams(
            collective_id=0, has_side_effects=True, vmem_limit_bytes=57 * 1024 * 1024
        ),
    )(
        samples.reshape(rows, length),
        jnp.asarray(forward_table(length, bins)),
        jnp.asarray(inverse_table(length, LAGS, 2 * bins, padded)),
        offsets,
        bad_mask,
    )
    return tuple(jnp.transpose(x, (1, 0, 2))[:, :, :width] for x in (corr, mirr))


def solution(mesh):
    return jax.shard_map(
        on_device,
        mesh=mesh,
        in_specs=(P("blk", "rep", None), P(None, "blk"), P("blk")),
        out_specs=(P("blk", None, None), P("blk", None, None)),
        check_vma=False,
    )
```

```python
import functools
import math

import jax
import jax.numpy as jnp
import ml_dtypes
import numpy as np
from jax import lax
from jax.experimental import pallas as pl
from jax.experimental.pallas import tpu as pltpu
from jax.sharding import PartitionSpec as P

LAGS = 128
LANES = 128
AHEAD = 3
SUB = 8
PIECES = 4
MESH = pl.DeviceIdType.MESH
F32 = jnp.float32
BF16 = jnp.bfloat16


def forward_table(length, bins):
    phase = np.arange(length)[:, None] * np.arange(length // 2)[None, :] % length
    angle = phase * (2.0 * math.pi / length)
    real = np.cos(angle).reshape(length, -1, bins)
    imag = -np.sin(angle).reshape(length, -1, bins)
    both = np.concatenate([real, imag], axis=2).reshape(length, -1, 4 * bins).transpose(1, 0, 2)
    return np.ascontiguousarray(both).astype(ml_dtypes.bfloat16)


def inverse_table(length, lag_half, bins, padded):
    width = 2 * lag_half + 1
    lag_idx = np.arange(width) - lag_half
    phase = np.arange(length // 2)[:, None] * (lag_idx[None, :] % length) % length
    angle = phase * (2.0 * math.pi / length)
    whole = np.zeros((2, length // 2, padded), np.float32)
    whole[0, :, :width] = np.cos(angle)
    whole[1, :, :width] = np.sin(angle)
    high = whole.astype(ml_dtypes.bfloat16)
    low = (whole - high.astype(np.float32)).astype(ml_dtypes.bfloat16)
    both = np.stack([high, low], axis=1).reshape(2, 2, -1, bins, padded)
    return np.ascontiguousarray(both.transpose(2, 0, 1, 3, 4))


def sum_rows(tiles):
    row = lax.broadcasted_iota(jnp.int32, tiles[0].shape, 0)
    low = row < 4
    tiles = [
        jnp.where(low, tiles[i], tiles[i + 4]) + pltpu.roll(jnp.where(low, tiles[i + 4], tiles[i]), 4, 0)
        for i in range(4)
    ]
    low = lax.rem(row, 4) < 2
    tiles = [
        jnp.where(low, tiles[i] + pltpu.roll(tiles[i], 6, 0), tiles[i + 2] + pltpu.roll(tiles[i + 2], 2, 0))
        for i in range(2)
    ]
    low = lax.rem(row, 2) < 1
    return jnp.where(low, tiles[0] + pltpu.roll(tiles[0], 7, 0), tiles[1] + pltpu.roll(tiles[1], 1, 0))


def kernel(
    scale,
    groups,
    samples_in, table, back, offsets_in, bad_in,
    corr, mirr,
    samples, offsets, bad, in_sem, table_v, back_v, spec, norm, own, part, peer, even, odd_, flip,
    table_sem, back_sem, send_sem, recv_sem, rep_send, rep_recv, mir_send, mir_recv,
    *far_flat,
):
    stops, channels, padded = corr.shape
    rows = samples.shape[0]
    segs = rows // channels
    bins = own.shape[-1]
    far = [far_flat[d * groups:(d + 1) * groups] for d in range(stops)]
    blk, rep = lax.axis_index("blk"), lax.axis_index("rep")
    n = lax.axis_size("blk")
    core = lax.rem(blk, 2)
    odd = lax.rem(blk // 2, 2)
    up = lax.rem(blk + 4, n)
    beside = blk + 2 - 4 * odd
    sibling = blk + 1 - 2 * core
    other = 1 - rep

    def load(j):
        return pltpu.make_async_copy(table.at[j], table_v.at[j], table_sem.at[j])

    small = [
        pltpu.make_async_copy(samples_in, samples, in_sem.at[0]),
        pltpu.make_async_copy(bad_in, bad, in_sem.at[1]),
        pltpu.make_async_copy(offsets_in, offsets, in_sem.at[2]),
    ]
    small[0].start()
    load(0).start()
    small[1].start()
    small[2].start()
    for j in range(1, groups // 2):
        load(j).start()
    back_load = pltpu.make_async_copy(back, back_v, back_sem)

    barrier = pltpu.get_barrier_semaphore()
    for by in range(1, stops + 1):
        for who in (lax.rem(blk + by, n), lax.rem(blk + n - by, n)):
            pl.semaphore_signal(barrier, inc=1, device_id=(who, rep), device_id_type=MESH)
    pl.semaphore_signal(barrier, inc=1, device_id=(blk, other), device_id_type=MESH)

    def pieces(k):
        return PIECES if k == groups - 1 else PIECES // 2

    def send(src, stop, k, lane, who, piece=None):
        dst = far[stop - 1][k]
        if piece is not None and pieces(k) > 1:
            size = channels // pieces(k)
            src, dst = (ref.at[pl.ds(piece * size, size)] for ref in (src, dst))
        return pltpu.make_async_remote_copy(
            src_ref=src,
            dst_ref=dst,
            send_sem=send_sem.at[lane, k, piece or 0],
            recv_sem=recv_sem.at[stop - 1, k, piece or 0],
            device_id=(who, rep),
            device_id_type=MESH,
        )

    def arrived(stop, k, piece=None):
        send(own.at[k], stop, k, 0, up, piece).wait_recv()

    norm[...] = jnp.zeros_like(norm)
    small[0].wait()

    @pl.loop(0, groups // 2)
    def _(j):
        load(j).wait()
        got = jnp.dot(samples[...], table_v[j], preferred_element_type=F32)
        spec[2 * j] = got[:, :2 * bins]
        spec[2 * j + 1] = got[:, 2 * bins:]
        square = got * got
        norm[...] += (square[:, :bins] + square[:, bins:2 * bins]) + (square[:, 2 * bins:3 * bins] + square[:, 3 * bins:])

    back_load.start()
    power = jnp.sum(norm[...], axis=1, keepdims=True) / (groups * bins)
    norm[...] = jnp.broadcast_to(lax.rsqrt(power + 1e-06), norm.shape)
    small[1].wait()
    for c in range(channels):
        norm[c * segs:(c + 1) * segs, :] *= (1 - bad[c]).astype(F32)

    pl.semaphore_wait(barrier, 2 * stops + 1)

    def launch(k):
        for piece in range(pieces(k)):
            send(own.at[k], 4, k, 0, up, piece).start()

            @pl.when(odd == 0)
            def _():
                send(own.at[k], 2, k, 1, beside, piece).start()

        @pl.when(core == 0)
        def _():
            send(own.at[k], 1, k, 2, sibling).start()

    for k in range(groups):
        real = (spec[k, :, :bins] * norm[...]).reshape(channels, segs, bins)
        imag = (spec[k, :, bins:] * norm[...]).reshape(channels, segs, bins)
        own[k] = jnp.concatenate([real, imag], axis=1).astype(BF16)
        if k < AHEAD:
            launch(k)

    def exchange(k, d):
        return pltpu.make_async_remote_copy(
            src_ref=part.at[k, d],
            dst_ref=peer.at[k, d],
            send_sem=rep_send.at[k, d],
            recv_sem=rep_recv.at[k, d],
            device_id=(blk, other),
            device_id_type=MESH,
        )

    def pair_up(k, stop):
        d = stop - 1

        @pl.loop(0, channels // SUB)
        def _(octet):
            base = pl.multiple_of(octet * SUB, SUB)
            reals, imags = [], []
            for u in range(SUB):
                mine = own[k, base + u].astype(F32)
                theirs = far[d][k][offsets[d, base + u]].astype(F32)
                real_a, imag_a = mine[:segs], mine[segs:]
                real_b, imag_b = theirs[:segs], theirs[segs:]
                reals.append(real_a * real_b + imag_a * imag_b)
                imags.append(imag_a * real_b - real_a * imag_b)
            part[k, d, 0, pl.ds(base, SUB), :] = sum_rows(reals)
            part[k, d, 1, pl.ds(base, SUB), :] = sum_rows(imags)

        exchange(k, d).start()

    even[...] = jnp.zeros_like(even)
    odd_[...] = jnp.zeros_like(odd_)

    def finish(pair, stops_done):
        first, second = 2 * pair, 2 * pair + 1
        low_d, high_d = min(stops_done) - 1, max(stops_done)
        for d in range(low_d, high_d):
            exchange(first, d).wait_recv()
            exchange(second, d).wait_recv()
        count = (high_d - low_d) * channels
        held = pl.ds(low_d * channels, count)
        for side, total in ((0, even), (1, odd_)):
            cross = jnp.concatenate(
                [
                    (part[k, low_d:high_d, side] + peer[k, low_d:high_d, side]).reshape(count, bins)
                    for k in (first, second)
                ],
                axis=1,
            )
            high = cross.astype(BF16)
            low = (cross - high.astype(F32)).astype(BF16)
            total[held, :] += (
                jnp.dot(high, back_v[pair, side, 0], preferred_element_type=F32)
                + jnp.dot(low, back_v[pair, side, 0], preferred_element_type=F32)
                + jnp.dot(high, back_v[pair, side, 1], preferred_element_type=F32)
            )

    def go_home(d):
        return pltpu.make_async_remote_copy(
            src_ref=flip.at[d],
            dst_ref=mirr.at[d],
            send_sem=mir_send.at[d],
            recv_sem=mir_recv.at[d],
            device_id=(lax.rem(blk + n - d - 1, n), rep),
            device_id_type=MESH,
        )

    def conclude(stop):
        d = stop - 1
        finish(groups // 2 - 1, (stop,))
        held = pl.ds(d * channels, channels)
        flip[d] = (even[held, :] + odd_[held, :]) * scale
        go_home(d).start()
        corr[d] = (even[held, :] - odd_[held, :]) * scale

    back_load.wait()
    small[2].wait()
    for k in range(groups):
        for piece in range(pieces(k)):
            arrived(4, k, piece)

            @pl.when(odd == 1)
            def _():
                send(far[3][k], 2, k, 1, beside, piece).start()

        @pl.when(core == 1)
        def _():
            send(far[3][k], 3, k, 3, sibling).start()

        if k + AHEAD < groups:
            launch(k + AHEAD)
        pair_up(k, 4)
        for piece in range(pieces(k)):
            arrived(2, k, piece)

        @pl.when(core == 1)
        def _():
            send(far[1][k], 1, k, 2, sibling).start()

        @pl.when(core == 0)
        def _():
            send(far[1][k], 3, k, 3, sibling).start()

        pair_up(k, 2)
        for stop in (3, 1):
            arrived(stop, k)
            pair_up(k, stop)
            if k == groups - 1:
                conclude(4 if stop == 3 else 2)
        if k >= 2 and k % 2 == 0:
            finish(k // 2 - 1, range(1, stops + 1))
    conclude(3)
    conclude(1)
    for k in range(groups):
        for lane in range(4):
            for piece in range(pieces(k) if lane < 2 else 1):
                send(own.at[k], 4, k, lane, up, piece if lane < 2 else None).wait_send()
        for d in range(stops):
            exchange(k, d).wait_send()
    for d in range(stops):
        go_home(d).wait()


def on_device(samples, offsets, bad_mask):
    channels, segs, length = samples.shape
    stops = offsets.shape[0]
    rows = channels * segs
    bins = LANES
    assert segs == SUB and channels % SUB == 0
    groups = length // 2 // bins
    width = 2 * LAGS + 1
    padded = -(-width // LANES) * LANES
    scale = 1.0 / math.sqrt(segs * lax.axis_size("rep") * (length // 2))
    vmem = pl.BlockSpec(memory_space=pltpu.VMEM)
    hbm = pl.BlockSpec(memory_space=pl.ANY)
    out = pltpu.VMEM((stops, channels, padded), F32)
    dma = pltpu.SemaphoreType.DMA
    corr, mirr = pl.pallas_call(
        functools.partial(kernel, scale, groups),
        out_shape=(out, out),
        in_specs=[hbm] * 5,
        out_specs=(vmem, vmem),
        scratch_shapes=[
            pltpu.VMEM((rows, length), BF16),
            pltpu.SMEM((stops, channels), jnp.int32),
            pltpu.SMEM((channels,), jnp.int32),
            dma((3,)),
            pltpu.VMEM((groups // 2, length, 4 * bins), BF16),
            pltpu.VMEM((groups // 2, 2, 2, 2 * bins, padded), BF16),
            pltpu.VMEM((groups, rows, 2 * bins), F32),
            pltpu.VMEM((rows, bins), F32),
            pltpu.VMEM((groups, channels, 2 * segs, bins), BF16),
            pltpu.VMEM((groups, stops, 2, channels, bins), F32),
            pltpu.VMEM((groups, stops, 2, channels, bins), F32),
            pltpu.VMEM((stops * channels, padded), F32),
            pltpu.VMEM((stops * channels, padded), F32),
            pltpu.VMEM((stops, channels, padded), F32),
            dma((groups // 2,)), dma,
            dma((4, groups, PIECES)), dma((stops, groups, PIECES)),
            dma((groups, stops)), dma((groups, stops)),
            dma((stops,)), dma((stops,)),
        ] + [pltpu.VMEM((channels, 2 * segs, bins), BF16)] * (stops * groups),
        compiler_params=pltpu.CompilerParams(
            collective_id=0, has_side_effects=True, vmem_limit_bytes=57 * 1024 * 1024
        ),
    )(
        samples.reshape(rows, length),
        jnp.asarray(forward_table(length, bins)),
        jnp.asarray(inverse_table(length, LAGS, 2 * bins, padded)),
        offsets,
        bad_mask,
    )
    return tuple(jnp.transpose(x, (1, 0, 2))[:, :, :width] for x in (corr, mirr))


def solution(mesh):
    return jax.shard_map(
        on_device,
        mesh=mesh,
        in_specs=(P("blk", "rep", None), P(None, "blk"), P("blk")),
        out_specs=(P("blk", None, None), P("blk", None, None)),
        check_vma=False,
    )
```

```python
import functools
import math

import jax
import jax.numpy as jnp
import ml_dtypes
import numpy as np
from jax import lax
from jax.experimental import pallas as pl
from jax.experimental.pallas import tpu as pltpu
from jax.sharding import PartitionSpec as P

LAGS = 128
LANES = 128
AHEAD = 4
SUB = 8
PIECES = 4
MESH = pl.DeviceIdType.MESH
F32 = jnp.float32
BF16 = jnp.bfloat16


def forward_table(length, bins):
    phase = np.arange(length)[:, None] * np.arange(length // 2)[None, :] % length
    angle = phase * (2.0 * math.pi / length)
    real = np.cos(angle).reshape(length, -1, bins)
    imag = -np.sin(angle).reshape(length, -1, bins)
    both = np.concatenate([real, imag], axis=2).reshape(length, -1, 4 * bins).transpose(1, 0, 2)
    return np.ascontiguousarray(both).astype(ml_dtypes.bfloat16)


def inverse_table(length, lag_half, bins, padded):
    width = 2 * lag_half + 1
    lag_idx = np.arange(width) - lag_half
    phase = np.arange(length // 2)[:, None] * (lag_idx[None, :] % length) % length
    angle = phase * (2.0 * math.pi / length)
    whole = np.zeros((2, length // 2, padded), np.float32)
    whole[0, :, :width] = np.cos(angle)
    whole[1, :, :width] = np.sin(angle)
    high = whole.astype(ml_dtypes.bfloat16)
    low = (whole - high.astype(np.float32)).astype(ml_dtypes.bfloat16)
    both = np.stack([high, low], axis=1).reshape(2, 2, -1, bins, padded)
    return np.ascontiguousarray(both.transpose(2, 0, 1, 3, 4))


def sum_rows(tiles):
    row = lax.broadcasted_iota(jnp.int32, tiles[0].shape, 0)
    low = row < 4
    tiles = [
        jnp.where(low, tiles[i], tiles[i + 4]) + pltpu.roll(jnp.where(low, tiles[i + 4], tiles[i]), 4, 0)
        for i in range(4)
    ]
    low = lax.rem(row, 4) < 2
    tiles = [
        jnp.where(low, tiles[i] + pltpu.roll(tiles[i], 6, 0), tiles[i + 2] + pltpu.roll(tiles[i + 2], 2, 0))
        for i in range(2)
    ]
    low = lax.rem(row, 2) < 1
    return jnp.where(low, tiles[0] + pltpu.roll(tiles[0], 7, 0), tiles[1] + pltpu.roll(tiles[1], 1, 0))


def kernel(
    scale,
    groups,
    samples_in, table, back, offsets_in, bad_in,
    corr, mirr,
    samples, offsets, bad, in_sem, table_v, back_v, spec, norm, own, part, peer, even, odd_, flip,
    table_sem, back_sem, send_sem, recv_sem, rep_send, rep_recv, mir_send, mir_recv,
    *far_flat,
):
    stops, channels, padded = corr.shape
    rows = samples.shape[0]
    segs = rows // channels
    bins = own.shape[-1]
    far = [far_flat[d * groups:(d + 1) * groups] for d in range(stops)]
    blk, rep = lax.axis_index("blk"), lax.axis_index("rep")
    n = lax.axis_size("blk")
    core = lax.rem(blk, 2)
    odd = lax.rem(blk // 2, 2)
    up = lax.rem(blk + 4, n)
    beside = blk + 2 - 4 * odd
    sibling = blk + 1 - 2 * core
    other = 1 - rep

    def load(j):
        return pltpu.make_async_copy(table.at[j], table_v.at[j], table_sem.at[j])

    small = [
        pltpu.make_async_copy(samples_in, samples, in_sem.at[0]),
        pltpu.make_async_copy(bad_in, bad, in_sem.at[1]),
        pltpu.make_async_copy(offsets_in, offsets, in_sem.at[2]),
    ]
    small[0].start()
    load(0).start()
    small[1].start()
    small[2].start()
    for j in range(1, groups // 2):
        load(j).start()
    back_load = pltpu.make_async_copy(back, back_v, back_sem)

    barrier = pltpu.get_barrier_semaphore()
    for by in range(1, stops + 1):
        for who in (lax.rem(blk + by, n), lax.rem(blk + n - by, n)):
            pl.semaphore_signal(barrier, inc=1, device_id=(who, rep), device_id_type=MESH)
    pl.semaphore_signal(barrier, inc=1, device_id=(blk, other), device_id_type=MESH)

    def pieces(k):
        return PIECES if k == groups - 1 else PIECES // 2

    def send(src, stop, k, lane, who, piece=None):
        dst = far[stop - 1][k]
        if piece is not None and pieces(k) > 1:
            size = channels // pieces(k)
            src, dst = (ref.at[pl.ds(piece * size, size)] for ref in (src, dst))
        return pltpu.make_async_remote_copy(
            src_ref=src,
            dst_ref=dst,
            send_sem=send_sem.at[lane, k, piece or 0],
            recv_sem=recv_sem.at[stop - 1, k, piece or 0],
            device_id=(who, rep),
            device_id_type=MESH,
        )

    def arrived(stop, k, piece=None):
        send(own.at[k], stop, k, 0, up, piece).wait_recv()

    norm[...] = jnp.zeros_like(norm)
    small[0].wait()

    @pl.loop(0, groups // 2, unroll=True)
    def _(j):
        load(j).wait()
        got = jnp.dot(samples[...], table_v[j], preferred_element_type=F32)
        spec[2 * j] = got[:, :2 * bins]
        spec[2 * j + 1] = got[:, 2 * bins:]
        square = got * got
        norm[...] += (square[:, :bins] + square[:, bins:2 * bins]) + (square[:, 2 * bins:3 * bins] + square[:, 3 * bins:])

    back_load.start()
    power = jnp.sum(norm[...], axis=1, keepdims=True) / (groups * bins)
    norm[...] = jnp.broadcast_to(lax.rsqrt(power + 1e-06), norm.shape)
    small[1].wait()
    for c in range(channels):
        norm[c * segs:(c + 1) * segs, :] *= (1 - bad[c]).astype(F32)

    pl.semaphore_wait(barrier, 2 * stops + 1)

    def launch(k):
        for piece in range(pieces(k)):
            send(own.at[k], 4, k, 0, up, piece).start()

            @pl.when(odd == 0)
            def _():
                send(own.at[k], 2, k, 1, beside, piece).start()

        @pl.when(core == 0)
        def _():
            send(own.at[k], 1, k, 2, sibling).start()

    for k in range(groups):
        real = (spec[k, :, :bins] * norm[...]).reshape(channels, segs, bins)
        imag = (spec[k, :, bins:] * norm[...]).reshape(channels, segs, bins)
        own[k] = jnp.concatenate([real, imag], axis=1).astype(BF16)
        if k < AHEAD:
            launch(k)

    def exchange(k, d):
        return pltpu.make_async_remote_copy(
            src_ref=part.at[k, d],
            dst_ref=peer.at[k, d],
            send_sem=rep_send.at[k, d],
            recv_sem=rep_recv.at[k, d],
            device_id=(blk, other),
            device_id_type=MESH,
        )

    def pair_up(k, stop):
        d = stop - 1

        @pl.loop(0, channels // SUB)
        def _(octet):
            base = pl.multiple_of(octet * SUB, SUB)
            reals, imags = [], []
            for u in range(SUB):
                mine = own[k, base + u].astype(F32)
                theirs = far[d][k][offsets[d, base + u]].astype(F32)
                real_a, imag_a = mine[:segs], mine[segs:]
                real_b, imag_b = theirs[:segs], theirs[segs:]
                reals.append(real_a * real_b + imag_a * imag_b)
                imags.append(imag_a * real_b - real_a * imag_b)
            part[k, d, 0, pl.ds(base, SUB), :] = sum_rows(reals)
            part[k, d, 1, pl.ds(base, SUB), :] = sum_rows(imags)

        exchange(k, d).start()

    even[...] = jnp.zeros_like(even)
    odd_[...] = jnp.zeros_like(odd_)

    def finish(pair, stops_done):
        first, second = 2 * pair, 2 * pair + 1
        low_d, high_d = min(stops_done) - 1, max(stops_done)
        for d in range(low_d, high_d):
            exchange(first, d).wait_recv()
            exchange(second, d).wait_recv()
        count = (high_d - low_d) * channels
        held = pl.ds(low_d * channels, count)
        for side, total in ((0, even), (1, odd_)):
            cross = jnp.concatenate(
                [
                    (part[k, low_d:high_d, side] + peer[k, low_d:high_d, side]).reshape(count, bins)
                    for k in (first, second)
                ],
                axis=1,
            )
            high = cross.astype(BF16)
            low = (cross - high.astype(F32)).astype(BF16)
            total[held, :] += (
                jnp.dot(high, back_v[pair, side, 0], preferred_element_type=F32)
                + jnp.dot(low, back_v[pair, side, 0], preferred_element_type=F32)
                + jnp.dot(high, back_v[pair, side, 1], preferred_element_type=F32)
            )

    def go_home(d):
        return pltpu.make_async_remote_copy(
            src_ref=flip.at[d],
            dst_ref=mirr.at[d],
            send_sem=mir_send.at[d],
            recv_sem=mir_recv.at[d],
            device_id=(lax.rem(blk + n - d - 1, n), rep),
            device_id_type=MESH,
        )

    def conclude(stop):
        d = stop - 1
        finish(groups // 2 - 1, (stop,))
        held = pl.ds(d * channels, channels)
        flip[d] = (even[held, :] + odd_[held, :]) * scale
        go_home(d).start()
        corr[d] = (even[held, :] - odd_[held, :]) * scale

    back_load.wait()
    small[2].wait()
    for k in range(groups):
        if k + AHEAD < groups:
            launch(k + AHEAD)
        for piece in range(pieces(k)):
            arrived(4, k, piece)

            @pl.when(odd == 1)
            def _():
                send(far[3][k], 2, k, 1, beside, piece).start()

        @pl.when(core == 1)
        def _():
            send(far[3][k], 3, k, 3, sibling).start()

        pair_up(k, 4)
        for piece in range(pieces(k)):
            arrived(2, k, piece)

        @pl.when(core == 1)
        def _():
            send(far[1][k], 1, k, 2, sibling).start()

        @pl.when(core == 0)
        def _():
            send(far[1][k], 3, k, 3, sibling).start()

        pair_up(k, 2)
        for stop in (3, 1):
            arrived(stop, k)
            pair_up(k, stop)
            if k == groups - 1:
                conclude(4 if stop == 3 else 2)
        if k >= 2 and k % 2 == 0:
            finish(k // 2 - 1, range(1, stops + 1))
    conclude(3)
    conclude(1)
    for k in range(groups):
        for lane in range(4):
            for piece in range(pieces(k) if lane < 2 else 1):
                send(own.at[k], 4, k, lane, up, piece if lane < 2 else None).wait_send()
        for d in range(stops):
            exchange(k, d).wait_send()
    for d in range(stops):
        go_home(d).wait()


def on_device(samples, offsets, bad_mask):
    channels, segs, length = samples.shape
    stops = offsets.shape[0]
    rows = channels * segs
    bins = LANES
    assert segs == SUB and channels % SUB == 0
    groups = length // 2 // bins
    width = 2 * LAGS + 1
    padded = -(-width // LANES) * LANES
    scale = 1.0 / math.sqrt(segs * lax.axis_size("rep") * (length // 2))
    vmem = pl.BlockSpec(memory_space=pltpu.VMEM)
    hbm = pl.BlockSpec(memory_space=pl.ANY)
    out = pltpu.VMEM((stops, channels, padded), F32)
    dma = pltpu.SemaphoreType.DMA
    corr, mirr = pl.pallas_call(
        functools.partial(kernel, scale, groups),
        out_shape=(out, out),
        in_specs=[hbm] * 5,
        out_specs=(vmem, vmem),
        scratch_shapes=[
            pltpu.VMEM((rows, length), BF16),
            pltpu.SMEM((stops, channels), jnp.int32),
            pltpu.SMEM((channels,), jnp.int32),
            dma((3,)),
            pltpu.VMEM((groups // 2, length, 4 * bins), BF16),
            pltpu.VMEM((groups // 2, 2, 2, 2 * bins, padded), BF16),
            pltpu.VMEM((groups, rows, 2 * bins), F32),
            pltpu.VMEM((rows, bins), F32),
            pltpu.VMEM((groups, channels, 2 * segs, bins), BF16),
            pltpu.VMEM((groups, stops, 2, channels, bins), F32),
            pltpu.VMEM((groups, stops, 2, channels, bins), F32),
            pltpu.VMEM((stops * channels, padded), F32),
            pltpu.VMEM((stops * channels, padded), F32),
            pltpu.VMEM((stops, channels, padded), F32),
            dma((groups // 2,)), dma,
            dma((4, groups, PIECES)), dma((stops, groups, PIECES)),
            dma((groups, stops)), dma((groups, stops)),
            dma((stops,)), dma((stops,)),
        ] + [pltpu.VMEM((channels, 2 * segs, bins), BF16)] * (stops * groups),
        compiler_params=pltpu.CompilerParams(
            collective_id=0, has_side_effects=True, vmem_limit_bytes=57 * 1024 * 1024
        ),
    )(
        samples.reshape(rows, length),
        jnp.asarray(forward_table(length, bins)),
        jnp.asarray(inverse_table(length, LAGS, 2 * bins, padded)),
        offsets,
        bad_mask,
    )
    return tuple(jnp.transpose(x, (1, 0, 2))[:, :, :width] for x in (corr, mirr))


def solution(mesh):
    return jax.shard_map(
        on_device,
        mesh=mesh,
        in_specs=(P("blk", "rep", None), P(None, "blk"), P("blk")),
        out_specs=(P("blk", None, None), P("blk", None, None)),
        check_vma=False,
    )
```

```python
import functools
import math

import jax
import jax.numpy as jnp
import ml_dtypes
import numpy as np
from jax import lax
from jax.experimental import pallas as pl
from jax.experimental.pallas import tpu as pltpu
from jax.sharding import PartitionSpec as P

LAGS = 128
LANES = 128
AHEAD = 4
SUB = 8
PIECES = 4
MESH = pl.DeviceIdType.MESH
F32 = jnp.float32
BF16 = jnp.bfloat16


def forward_table(length, bins):
    phase = np.arange(length)[:, None] * np.arange(length // 2)[None, :] % length
    angle = phase * (2.0 * math.pi / length)
    real = np.cos(angle).reshape(length, -1, bins)
    imag = -np.sin(angle).reshape(length, -1, bins)
    both = np.concatenate([real, imag], axis=2).reshape(length, -1, 4 * bins).transpose(1, 0, 2)
    return np.ascontiguousarray(both).astype(ml_dtypes.bfloat16)


def inverse_table(length, lag_half, bins, padded):
    width = 2 * lag_half + 1
    lag_idx = np.arange(width) - lag_half
    phase = np.arange(length // 2)[:, None] * (lag_idx[None, :] % length) % length
    angle = phase * (2.0 * math.pi / length)
    whole = np.zeros((2, length // 2, padded), np.float32)
    whole[0, :, :width] = np.cos(angle)
    whole[1, :, :width] = np.sin(angle)
    high = whole.astype(ml_dtypes.bfloat16)
    low = (whole - high.astype(np.float32)).astype(ml_dtypes.bfloat16)
    both = np.stack([high, low], axis=1).reshape(2, 2, -1, bins, padded)
    return np.ascontiguousarray(both.transpose(2, 0, 1, 3, 4))


def sum_rows(tiles):
    row = lax.broadcasted_iota(jnp.int32, tiles[0].shape, 0)
    low = row < 4
    tiles = [
        jnp.where(low, tiles[i], tiles[i + 4]) + pltpu.roll(jnp.where(low, tiles[i + 4], tiles[i]), 4, 0)
        for i in range(4)
    ]
    low = lax.rem(row, 4) < 2
    tiles = [
        jnp.where(low, tiles[i] + pltpu.roll(tiles[i], 6, 0), tiles[i + 2] + pltpu.roll(tiles[i + 2], 2, 0))
        for i in range(2)
    ]
    low = lax.rem(row, 2) < 1
    return jnp.where(low, tiles[0] + pltpu.roll(tiles[0], 7, 0), tiles[1] + pltpu.roll(tiles[1], 1, 0))


def kernel(
    scale,
    groups,
    samples_in, table, back, offsets_in, bad_in,
    corr, mirr,
    samples, offsets, bad, in_sem, table_v, back_v, spec, norm, own, part, peer, even, odd_, flip,
    table_sem, back_sem, send_sem, recv_sem, rep_send, rep_recv, mir_send, mir_recv,
    *far_flat,
):
    stops, channels, padded = corr.shape
    rows = samples.shape[0]
    segs = rows // channels
    bins = own.shape[-1]
    far = [far_flat[d * groups:(d + 1) * groups] for d in range(stops)]
    blk, rep = lax.axis_index("blk"), lax.axis_index("rep")
    n = lax.axis_size("blk")
    core = lax.rem(blk, 2)
    odd = lax.rem(blk // 2, 2)
    up = lax.rem(blk + 4, n)
    beside = blk + 2 - 4 * odd
    sibling = blk + 1 - 2 * core
    other = 1 - rep

    def load(j):
        return pltpu.make_async_copy(table.at[j], table_v.at[j], table_sem.at[j])

    small = [
        pltpu.make_async_copy(samples_in, samples, in_sem.at[0]),
        pltpu.make_async_copy(bad_in, bad, in_sem.at[1]),
        pltpu.make_async_copy(offsets_in, offsets, in_sem.at[2]),
    ]
    small[0].start()
    load(0).start()
    small[1].start()
    small[2].start()
    for j in range(1, groups // 2):
        load(j).start()
    back_load = pltpu.make_async_copy(back, back_v, back_sem)

    barrier = pltpu.get_barrier_semaphore()
    for by in range(1, stops + 1):
        for who in (lax.rem(blk + by, n), lax.rem(blk + n - by, n)):
            pl.semaphore_signal(barrier, inc=1, device_id=(who, rep), device_id_type=MESH)
    pl.semaphore_signal(barrier, inc=1, device_id=(blk, other), device_id_type=MESH)

    def pieces(k):
        return PIECES

    def send(src, stop, k, lane, who, piece=None):
        dst = far[stop - 1][k]
        if piece is not None and pieces(k) > 1:
            size = channels // pieces(k)
            src, dst = (ref.at[pl.ds(piece * size, size)] for ref in (src, dst))
        return pltpu.make_async_remote_copy(
            src_ref=src,
            dst_ref=dst,
            send_sem=send_sem.at[lane, k, piece or 0],
            recv_sem=recv_sem.at[stop - 1, k, piece or 0],
            device_id=(who, rep),
            device_id_type=MESH,
        )

    def arrived(stop, k, piece=None):
        send(own.at[k], stop, k, 0, up, piece).wait_recv()

    norm[...] = jnp.zeros_like(norm)
    small[0].wait()

    @pl.loop(0, groups // 2, unroll=True)
    def _(j):
        load(j).wait()
        got = jnp.dot(samples[...], table_v[j], preferred_element_type=F32)
        spec[2 * j] = got[:, :2 * bins]
        spec[2 * j + 1] = got[:, 2 * bins:]
        square = got * got
        norm[...] += (square[:, :bins] + square[:, bins:2 * bins]) + (square[:, 2 * bins:3 * bins] + square[:, 3 * bins:])

    back_load.start()
    power = jnp.sum(norm[...], axis=1, keepdims=True) / (groups * bins)
    norm[...] = jnp.broadcast_to(lax.rsqrt(power + 1e-06), norm.shape)
    small[1].wait()
    for c in range(channels):
        norm[c * segs:(c + 1) * segs, :] *= (1 - bad[c]).astype(F32)

    pl.semaphore_wait(barrier, 2 * stops + 1)

    def launch(k):
        for piece in range(pieces(k)):
            send(own.at[k], 4, k, 0, up, piece).start()

            @pl.when(odd == 0)
            def _():
                send(own.at[k], 2, k, 1, beside, piece).start()

        @pl.when(core == 0)
        def _():
            send(own.at[k], 1, k, 2, sibling).start()

    for k in range(groups):
        real = (spec[k, :, :bins] * norm[...]).reshape(channels, segs, bins)
        imag = (spec[k, :, bins:] * norm[...]).reshape(channels, segs, bins)
        own[k] = jnp.concatenate([real, imag], axis=1).astype(BF16)
        if k < AHEAD:
            launch(k)

    def exchange(k, d):
        return pltpu.make_async_remote_copy(
            src_ref=part.at[k, d],
            dst_ref=peer.at[k, d],
            send_sem=rep_send.at[k, d],
            recv_sem=rep_recv.at[k, d],
            device_id=(blk, other),
            device_id_type=MESH,
        )

    def pair_up(k, stop):
        d = stop - 1

        @pl.loop(0, channels // SUB)
        def _(octet):
            base = pl.multiple_of(octet * SUB, SUB)
            reals, imags = [], []
            for u in range(SUB):
                mine = own[k, base + u].astype(F32)
                theirs = far[d][k][offsets[d, base + u]].astype(F32)
                real_a, imag_a = mine[:segs], mine[segs:]
                real_b, imag_b = theirs[:segs], theirs[segs:]
                reals.append(real_a * real_b + imag_a * imag_b)
                imags.append(imag_a * real_b - real_a * imag_b)
            part[k, d, 0, pl.ds(base, SUB), :] = sum_rows(reals)
            part[k, d, 1, pl.ds(base, SUB), :] = sum_rows(imags)

        exchange(k, d).start()

    even[...] = jnp.zeros_like(even)
    odd_[...] = jnp.zeros_like(odd_)

    def finish(pair, stops_done):
        first, second = 2 * pair, 2 * pair + 1
        low_d, high_d = min(stops_done) - 1, max(stops_done)
        for d in range(low_d, high_d):
            exchange(first, d).wait_recv()
            exchange(second, d).wait_recv()
        count = (high_d - low_d) * channels
        held = pl.ds(low_d * channels, count)
        for side, total in ((0, even), (1, odd_)):
            cross = jnp.concatenate(
                [
                    (part[k, low_d:high_d, side] + peer[k, low_d:high_d, side]).reshape(count, bins)
                    for k in (first, second)
                ],
                axis=1,
            )
            high = cross.astype(BF16)
            low = (cross - high.astype(F32)).astype(BF16)
            total[held, :] += (
                jnp.dot(high, back_v[pair, side, 0], preferred_element_type=F32)
                + jnp.dot(low, back_v[pair, side, 0], preferred_element_type=F32)
                + jnp.dot(high, back_v[pair, side, 1], preferred_element_type=F32)
            )

    def go_home(d):
        return pltpu.make_async_remote_copy(
            src_ref=flip.at[d],
            dst_ref=mirr.at[d],
            send_sem=mir_send.at[d],
            recv_sem=mir_recv.at[d],
            device_id=(lax.rem(blk + n - d - 1, n), rep),
            device_id_type=MESH,
        )

    def conclude(stop):
        d = stop - 1
        finish(groups // 2 - 1, (stop,))
        held = pl.ds(d * channels, channels)
        flip[d] = (even[held, :] + odd_[held, :]) * scale
        go_home(d).start()
        corr[d] = (even[held, :] - odd_[held, :]) * scale

    back_load.wait()
    small[2].wait()
    for k in range(groups):
        if k + AHEAD < groups:
            launch(k + AHEAD)
        for piece in range(pieces(k)):
            arrived(4, k, piece)

            @pl.when(odd == 1)
            def _():
                send(far[3][k], 2, k, 1, beside, piece).start()

        @pl.when(core == 1)
        def _():
            send(far[3][k], 3, k, 3, sibling).start()

        pair_up(k, 4)
        for piece in range(pieces(k)):
            arrived(2, k, piece)

        @pl.when(core == 1)
        def _():
            send(far[1][k], 1, k, 2, sibling).start()

        @pl.when(core == 0)
        def _():
            send(far[1][k], 3, k, 3, sibling).start()

        pair_up(k, 2)
        for stop in (3, 1):
            arrived(stop, k)
            pair_up(k, stop)
            if k == groups - 1:
                conclude(4 if stop == 3 else 2)
        if k >= 2 and k % 2 == 0:
            finish(k // 2 - 1, range(1, stops + 1))
    conclude(3)
    conclude(1)
    for k in range(groups):
        for lane in range(4):
            for piece in range(pieces(k) if lane < 2 else 1):
                send(own.at[k], 4, k, lane, up, piece if lane < 2 else None).wait_send()
        for d in range(stops):
            exchange(k, d).wait_send()
    for d in range(stops):
        go_home(d).wait()


def on_device(samples, offsets, bad_mask):
    channels, segs, length = samples.shape
    stops = offsets.shape[0]
    rows = channels * segs
    bins = LANES
    assert segs == SUB and channels % SUB == 0
    groups = length // 2 // bins
    width = 2 * LAGS + 1
    padded = -(-width // LANES) * LANES
    scale = 1.0 / math.sqrt(segs * lax.axis_size("rep") * (length // 2))
    vmem = pl.BlockSpec(memory_space=pltpu.VMEM)
    hbm = pl.BlockSpec(memory_space=pl.ANY)
    out = pltpu.VMEM((stops, channels, padded), F32)
    dma = pltpu.SemaphoreType.DMA
    corr, mirr = pl.pallas_call(
        functools.partial(kernel, scale, groups),
        out_shape=(out, out),
        in_specs=[hbm] * 5,
        out_specs=(vmem, vmem),
        scratch_shapes=[
            pltpu.VMEM((rows, length), BF16),
            pltpu.SMEM((stops, channels), jnp.int32),
            pltpu.SMEM((channels,), jnp.int32),
            dma((3,)),
            pltpu.VMEM((groups // 2, length, 4 * bins), BF16),
            pltpu.VMEM((groups // 2, 2, 2, 2 * bins, padded), BF16),
            pltpu.VMEM((groups, rows, 2 * bins), F32),
            pltpu.VMEM((rows, bins), F32),
            pltpu.VMEM((groups, channels, 2 * segs, bins), BF16),
            pltpu.VMEM((groups, stops, 2, channels, bins), F32),
            pltpu.VMEM((groups, stops, 2, channels, bins), F32),
            pltpu.VMEM((stops * channels, padded), F32),
            pltpu.VMEM((stops * channels, padded), F32),
            pltpu.VMEM((stops, channels, padded), F32),
            dma((groups // 2,)), dma,
            dma((4, groups, PIECES)), dma((stops, groups, PIECES)),
            dma((groups, stops)), dma((groups, stops)),
            dma((stops,)), dma((stops,)),
        ] + [pltpu.VMEM((channels, 2 * segs, bins), BF16)] * (stops * groups),
        compiler_params=pltpu.CompilerParams(
            collective_id=0, has_side_effects=True, vmem_limit_bytes=57 * 1024 * 1024
        ),
    )(
        samples.reshape(rows, length),
        jnp.asarray(forward_table(length, bins)),
        jnp.asarray(inverse_table(length, LAGS, 2 * bins, padded)),
        offsets,
        bad_mask,
    )
    return tuple(jnp.transpose(x, (1, 0, 2))[:, :, :width] for x in (corr, mirr))


def solution(mesh):
    return jax.shard_map(
        on_device,
        mesh=mesh,
        in_specs=(P("blk", "rep", None), P(None, "blk"), P("blk")),
        out_specs=(P("blk", None, None), P("blk", None, None)),
        check_vma=False,
    )
```
